256 devices in a mesh: group: 2 (over z_lo), row: 16 (over z_hi, x), col: 8 (over y, core).
Axes of the slice: x: 4, y: 4, z: 8 (z_hi: 4, z_lo: 2; z = z_hi * 2 + z_lo), core: 2. Of those that a mesh axis runs over, the one named last changes fastest.
Arguments:
- student_image: bfloat16 [32768, 768], P(('group', 'row', 'col')), may hold values from -32 to 32
- student_proj: bfloat16 [768, 512], replicated, may hold values from -1.1 to 1.1
- student_text: bfloat16 [32768, 512], P(('group', 'row', 'col')), may hold values from -4 to 4
- teacher_image: bfloat16 [32768, 1664], P(('group', 'col'), 'row'), may hold values from -32 to 32
- teacher_proj: bfloat16 [1664, 1280], P('row', 'col'), may hold values from -1.1 to 1.1
- teacher_text: bfloat16 [32768, 1280], P(('group', 'row', 'col')), may hold values from -4 to 4
- assignment: int32 [2, 16384], P('group', ('row', 'col')), may hold values from 0 to 16383, as said below
- pair_ids: int32 [2, 16384], P('group', ('row', 'col')), may hold values from 0 to 16383, each once within a row
Outputs:
- grad_embed: float32 [32768, 512], P(('group', 'row', 'col'))
- grad_proj: float32 [768, 512], replicated
The draws below stay inside these ranges and needn't reach their ends.
Inputs may be any that keep to these rules, and one draw needn't show every extreme that they name: `assignment`: within each sub-batch a permutation. The slots of the device at row r, col c of the layout take only teacher indices c * 16 * 128 to (c + 1) * 16 * 128 - 1, and exactly 8 of them from each run of 128 teacher indices there. `pair_ids`: each row a permutation.
All inputs are finite; a program needn't handle non-finite values.
Results may differ from the reference program's by a relative error of at most 0.0078.
Values may be sent and summed in bfloat16 or wider, within the bound.
A program may use at most 128 MiB of HBM per device.

```python
import math
import jax
import jax.numpy as jnp
from jax import lax

DT = 1664
ET = 1280
DS = 768
ES = 512
TOK_DEV = 128
SUB_BATCH = 16384
BATCH = 32768
N_GROUP = 2
N_ROW = 16
N_COL = 8


def common_image(key):
    return jnp.clip(jax.random.normal(jax.random.fold_in(key, 501), (BATCH, DS), jnp.float32), -4.0, 4.0)


def teacher_rows(key):
    return jnp.clip(jax.random.normal(jax.random.fold_in(key, 502), (BATCH, DT), jnp.float32), -4.0, 4.0)


def student_order(key):
    key = jax.random.fold_in(key, 503)
    first_key, second_key = jax.random.split(key)
    share_rows = TOK_DEV // N_ROW
    slots = jnp.arange(TOK_DEV, dtype=jnp.int32)
    shape_all = (N_GROUP, N_COL, N_ROW, TOK_DEV)
    first_scores = jax.random.randint(first_key, shape_all, 0, 1048576) * TOK_DEV + slots
    sources = (slots // share_rows)[jnp.argsort(first_scores, axis=-1)]
    second_scores = jax.random.randint(second_key, shape_all, 0, 1048576) * TOK_DEV + slots
    shuffles = jnp.argsort(second_scores, axis=-1).astype(jnp.int32)
    earlier = slots[None, :] < slots[:, None]
    same_source = sources[..., :, None] == sources[..., None, :]
    ranks = jnp.sum(same_source & earlier, axis=-1).astype(jnp.int32)
    group_ids = jnp.arange(N_GROUP, dtype=jnp.int32)[:, None, None, None]
    column_ids = jnp.arange(N_COL, dtype=jnp.int32)[None, :, None, None]
    target_rows = jnp.arange(N_ROW, dtype=jnp.int32)[None, None, :, None]
    within = shuffles[group_ids, column_ids, sources, target_rows * share_rows + ranks]
    local = column_ids * (N_ROW * TOK_DEV) + sources * TOK_DEV + within
    return jnp.transpose(local, (0, 2, 1, 3)).reshape(N_GROUP, N_ROW * N_COL * TOK_DEV).astype(jnp.int32)


def draw_assignment(key, part):
    return student_order(key)


def draw_student_image(key, part):
    values = common_image(key)
    return values.astype(jnp.bfloat16)


def draw_student_text(key, part):
    key = jax.random.fold_in(key, 2)
    first_key = jax.random.fold_in(key, 0)
    drawn = jnp.clip(jax.random.normal(first_key, (BATCH, ES), jnp.float32), -4.0, 4.0)
    return drawn.astype(jnp.bfloat16)


def draw_student_proj(key, part):
    key = jax.random.fold_in(key, 3)
    values = jnp.clip(jax.random.normal(key, (DS, ES), jnp.float32), -6.0, 6.0) / jnp.sqrt(float(DS))
    return values.astype(jnp.bfloat16)


def draw_teacher_image(key, part):
    values = teacher_rows(key)
    return values.astype(jnp.bfloat16)


def draw_teacher_proj(key, part):
    key = jax.random.fold_in(key, 6)
    values = jnp.clip(jax.random.normal(key, (DT, ET), jnp.float32), -6.0, 6.0) / jnp.sqrt(float(DT))
    return values.astype(jnp.bfloat16)


def draw_teacher_text(key, part):
    key = jax.random.fold_in(key, 5)
    first_key = jax.random.fold_in(key, 0)
    drawn = jnp.clip(jax.random.normal(first_key, (BATCH, ET), jnp.float32), -4.0, 4.0)
    return drawn.astype(jnp.bfloat16)


def setup_inputs(seed: int = 0) -> dict:
    key_list = jax.random.split(jax.random.key(seed), 9)
    student_image = draw_student_image(jax.random.fold_in(key_list[8], 71), 0)
    student_proj = draw_student_proj(jax.random.fold_in(key_list[8], 71), 0)
    student_text = draw_student_text(jax.random.fold_in(key_list[8], 71), 0)
    teacher_image = draw_teacher_image(jax.random.fold_in(key_list[8], 71), 0)
    teacher_proj = draw_teacher_proj(jax.random.fold_in(key_list[8], 71), 0)
    teacher_text = draw_teacher_text(jax.random.fold_in(key_list[8], 71), 0)
    assignment = draw_assignment(jax.random.fold_in(key_list[8], 71), 0)
    pair_ids = jax.vmap(lambda own: jax.random.permutation(own, SUB_BATCH))(jax.random.split(key_list[7], N_GROUP)).reshape((N_GROUP, SUB_BATCH)).astype(jnp.int32)
    return dict(student_image=student_image, student_proj=student_proj, student_text=student_text, teacher_image=teacher_image, teacher_proj=teacher_proj, teacher_text=teacher_text, assignment=assignment, pair_ids=pair_ids)


logit_scale = 100.0
norm_eps = 1e-06

def unit_rows(values):
    return values * lax.rsqrt(lax.optimization_barrier(jnp.sum(values * values, axis=1, keepdims=True)) + norm_eps)

def merge_stats(earlier, later):
    merged = []
    for position in range(0, len(earlier), 2):
        highest = jnp.maximum(earlier[position], later[position])
        combined = earlier[position + 1] * jnp.exp(earlier[position] - highest) + later[position + 1] * jnp.exp(later[position] - highest)
        merged += [highest, combined]
    return tuple(merged)

def affinity_grad(student_embed, text_unit, relaid, teacher_unit, pairs):
    row_count = student_embed.shape[0]
    block_rows = math.gcd(row_count, 512)
    steps_total = row_count // block_rows
    text_ids = jnp.arange(row_count, dtype=jnp.int32)

    def scores(position):
        start = (position * block_rows).astype(jnp.int32)
        image_block = lax.dynamic_slice_in_dim(student_embed, start, block_rows, 0)
        teacher_block = lax.dynamic_slice_in_dim(relaid, start, block_rows, 0)
        student_scores = logit_scale * jnp.dot(image_block, text_unit.T, preferred_element_type=jnp.float32)
        teacher_scores = logit_scale * jnp.dot(teacher_block, teacher_unit.T, preferred_element_type=jnp.float32)
        return (student_scores, teacher_scores)

    def first_pass(running, position):
        student_scores, teacher_scores = scores(position)
        block_stats = []
        row_lse = []
        for values in (student_scores, teacher_scores):
            highest = lax.optimization_barrier(jnp.max(values, axis=0))
            block_stats += [highest, lax.optimization_barrier(jnp.sum(jnp.exp(values - highest[None, :]), axis=0))]
            row_high = lax.optimization_barrier(jnp.max(values, axis=1))
            row_lse.append(row_high + jnp.log(lax.optimization_barrier(jnp.sum(jnp.exp(values - row_high[:, None]), axis=1))))
        return (merge_stats(running, tuple(block_stats)), tuple(row_lse))
    lowest = jnp.full((row_count,), -jnp.inf, jnp.float32)
    empty = jnp.zeros((row_count,), jnp.float32)
    column_stats, row_parts = lax.scan(first_pass, (lowest, empty, lowest, empty), jnp.arange(steps_total, dtype=jnp.int32))
    student_row = row_parts[0].reshape(row_count)
    teacher_row = row_parts[1].reshape(row_count)
    student_col = column_stats[0] + jnp.log(column_stats[1])
    teacher_col = column_stats[2] + jnp.log(column_stats[3])

    def second_pass(position):
        student_scores, teacher_scores = scores(position)
        start = (position * block_rows).astype(jnp.int32)
        srow = lax.dynamic_slice_in_dim(student_row, start, block_rows, 0)
        trow = lax.dynamic_slice_in_dim(teacher_row, start, block_rows, 0)
        matched = (lax.dynamic_slice_in_dim(pairs, start, block_rows, 0)[:, None] == text_ids[None, :]).astype(jnp.float32)
        weights = (2.0 * jnp.exp(student_scores - srow[:, None]) + 2.0 * jnp.exp(student_scores - student_col[None, :]) - jnp.exp(teacher_scores - trow[:, None]) - jnp.exp(teacher_scores - teacher_col[None, :]) - 2.0 * matched) / N_GROUP
        return logit_scale * jnp.dot(weights.astype(jnp.bfloat16), text_unit, preferred_element_type=jnp.float32)
    return lax.map(second_pass, jnp.arange(steps_total, dtype=jnp.int32)).reshape(row_count, -1)

def reference(student_image, student_proj, student_text, teacher_image, teacher_proj, teacher_text, assignment, pair_ids):
    raw_student = jnp.dot(student_image, student_proj, preferred_element_type=jnp.float32)
    student_unit = unit_rows(raw_student)
    student_embed = student_unit.astype(jnp.bfloat16)
    text_unit = unit_rows(student_text.astype(jnp.float32)).astype(jnp.bfloat16)
    teacher_raw = jnp.dot(teacher_image, teacher_proj, preferred_element_type=jnp.float32)
    teacher_embed = unit_rows(teacher_raw).astype(jnp.bfloat16)
    teacher_unit = unit_rows(teacher_text.astype(jnp.float32)).astype(jnp.bfloat16)
    pieces = []
    for subset in range(N_GROUP):
        offset = subset * SUB_BATCH
        relaid = teacher_embed[offset + assignment[subset]]
        pieces.append(affinity_grad(student_embed[offset:offset + SUB_BATCH], text_unit[offset:offset + SUB_BATCH], relaid, teacher_unit[offset:offset + SUB_BATCH], pair_ids[subset]))
    embed_grad = jnp.concatenate(pieces, 0)
    inner_term = lax.optimization_barrier(jnp.sum(student_unit * embed_grad, axis=1, keepdims=True))
    grad_embed = (embed_grad - student_unit * inner_term) * lax.rsqrt(lax.optimization_barrier(jnp.sum(raw_student * raw_student, axis=1, keepdims=True)) + norm_eps)
    grad_proj = jnp.dot(student_image.T, grad_embed.astype(jnp.bfloat16), preferred_element_type=jnp.float32)
    return (grad_embed, grad_proj)
```

```python
import functools
import math

import jax
import jax.numpy as jnp
from jax import lax
from jax.experimental import pallas as pl
from jax.experimental.pallas import tpu as pltpu
from jax.sharding import PartitionSpec as P

logit_scale = 100.0
norm_eps = 1e-06
MESH = pl.DeviceIdType.MESH
ring = 4
n_row = 16
n_col = 8
nt_dims = (((1,), (1,)), ((), ()))
tn_dims = (((0,), (0,)), ((), ()))


def unit_rows(values):
    return values * lax.rsqrt(jnp.sum(values * values, axis=1, keepdims=True) + norm_eps)


def merge_stats(earlier, later):
    merged = []
    for position in range(0, len(earlier), 2):
        highest = jnp.maximum(earlier[position], later[position])
        combined = earlier[position + 1] * jnp.exp(earlier[position] - highest) + later[
            position + 1
        ] * jnp.exp(later[position] - highest)
        merged += [highest, combined]
    return tuple(merged)


def tile_scores(images, texts):
    return logit_scale * jnp.einsum("ik,jk->ij", images, texts, preferred_element_type=jnp.float32)


def row_partial(values):
    highest = jnp.max(values, axis=1)
    return (highest, jnp.sum(jnp.exp(values - highest[:, None]), axis=1))


def column_partial(values):
    highest = jnp.max(values, axis=0)
    return (highest, jnp.sum(jnp.exp(values - highest[None, :]), axis=0))


class Place:
    def __init__(self):
        self.row = lax.axis_index("row")
        self.col = lax.axis_index("col")
        self.z, self.x = self.row // ring, self.row % ring
        self.y, self.core = self.col // 2, self.col % 2

    def along_x(self, step):
        return (self.x + step + ring) % ring

    def along_y(self, step):
        return (self.y + step + ring) % ring

    def along_z(self, step):
        return (self.z + step + ring) % ring

    def to_x(self, step):
        return {"row": self.z * ring + self.along_x(step)}

    def to_z(self, step):
        return {"row": self.along_z(step) * ring + self.x}

    def to_y(self, step):
        return {"col": self.along_y(step) * 2 + self.core}

    def sibling(self):
        return {"col": self.y * 2 + 1 - self.core}


class Mail:
    def __init__(self, send_sem, recv_sem):
        self.send_sem, self.recv_sem = send_sem, recv_sem
        self.used = 0
        self.sent = []

    def push(self, src, dst, device):
        index = self.used
        self.used += 1
        copy = pltpu.make_async_remote_copy(
            src_ref=src,
            dst_ref=dst,
            send_sem=self.send_sem.at[index],
            recv_sem=self.recv_sem.at[index],
            device_id=device,
            device_id_type=MESH,
        )
        copy.start()
        self.sent.append(copy)
        return index, device

    def got(self, slot, ticket):
        index, device = ticket
        pltpu.make_async_remote_copy(
            src_ref=slot,
            dst_ref=slot,
            send_sem=self.send_sem.at[index],
            recv_sem=self.recv_sem.at[index],
            device_id=device,
            device_id_type=MESH,
        ).wait_recv()

    def finish(self):
        for copy in self.sent:
            copy.wait_send()


def greet(devices):
    barrier = pltpu.get_barrier_semaphore()
    for device in devices:
        pl.semaphore_signal(barrier, inc=1, device_id=device, device_id_type=MESH)
    pl.semaphore_wait(barrier, len(devices))


def all_peers(place):
    return [{"row": (place.row + step) % n_row} for step in range(1, n_row)] + [
        {"col": (place.col + step) % n_col} for step in range(1, n_col)
    ]


class AlongColumn:
    def __init__(self, mail, place, ref):
        self.mail, self.place, self.ref = mail, place, ref
        self.half = ref.shape[1] // 2

    def block(self, step, core):
        return self.place.along_y(step) * 2 + core

    def lower(self, index):
        return self.ref.at[index, pl.ds(0, self.half)]

    def upper(self, index):
        return self.ref.at[index, pl.ds(self.half, self.half)]

    def start(self):
        place, mail = self.place, self.mail
        own = self.ref.at[place.col]
        self.up = mail.push(own, own, place.to_y(1))
        self.down = mail.push(own, own, place.to_y(-1))
        self.over = [mail.push(own, own, place.sibling())]

    def forward(self):
        place, mail = self.place, self.mail
        below = self.block(-1, place.core)
        mail.got(self.ref.at[below], self.up)
        self.up_half = mail.push(self.lower(below), self.lower(below), place.to_y(1))
        self.over.append(mail.push(self.ref.at[below], self.ref.at[below], place.sibling()))
        above = self.block(1, place.core)
        mail.got(self.ref.at[above], self.down)
        self.down_half = mail.push(self.upper(above), self.upper(above), place.to_y(-1))
        self.over.append(mail.push(self.ref.at[above], self.ref.at[above], place.sibling()))

    def last(self):
        place, mail = self.place, self.mail
        far = self.block(2, place.core)
        mail.got(self.lower(far), self.up_half)
        self.over.append(mail.push(self.lower(far), self.lower(far), place.sibling()))
        mail.got(self.upper(far), self.down_half)
        self.over.append(mail.push(self.upper(far), self.upper(far), place.sibling()))

    def end(self):
        place, mail = self.place, self.mail
        other = 1 - place.core
        mail.got(self.ref.at[self.block(0, other)], self.over[0])
        mail.got(self.ref.at[self.block(-1, other)], self.over[1])
        mail.got(self.ref.at[self.block(1, other)], self.over[2])
        far = self.block(2, other)
        mail.got(self.lower(far), self.over[3])
        mail.got(self.upper(far), self.over[4])


def gather_kernel(
    si_ref,
    sp_ref,
    st_ref,
    ti_ref,
    pt_ref,
    tt_ref,
    order_ref,
    pair_ref,
    text_ref,
    img_s_ref,
    img_t_ref,
    pairs_ref,
    raw_ref,
    orders,
    feat_out,
    feat_in,
    proj,
    embed,
    send_sem,
    recv_sem,
):
    place = Place()
    mail = Mail(send_sem, recv_sem)
    row, col = place.row, place.col
    per_device = st_ref.shape[0]
    teacher_width = tt_ref.shape[1]
    proj[col, row] = pt_ref[...]
    orders[row] = order_ref[...]
    pairs_ref[col] = pair_ref[...]
    greet(all_peers(place))
    order_mail = [
        mail.push(order_ref, orders.at[row], {"row": (row + step) % n_row})
        for step in range(1, n_row)
    ]
    own_proj = proj.at[col, row]
    proj_x = [mail.push(own_proj, own_proj, place.to_x(step)) for step in range(1, ring)]
    text_ref[row, :, :teacher_width] = unit_rows(tt_ref[...].astype(jnp.float32)).astype(
        jnp.bfloat16
    )
    text_ref[row, :, teacher_width:] = unit_rows(st_ref[...].astype(jnp.float32)).astype(
        jnp.bfloat16
    )

    def block(along_z, along_x):
        return text_ref.at[place.along_z(along_z) * ring + place.along_x(along_x)]

    def part(along_z, along_x, start):
        half = per_device // 2
        index = place.along_z(along_z) * ring + place.along_x(along_x)
        return text_ref.at[index, pl.ds(start * half, half)]

    own_text = block(0, 0)
    right, left = {}, {}

    def spread(step):
        right[step] = mail.push(block(step, 0), block(step, 0), place.to_x(1))
        left[step] = mail.push(block(step, 0), block(step, 0), place.to_x(-1))

    spread(0)
    for step in range(1, ring):
        mail.got(proj.at[col, place.z * ring + place.along_x(-step)], proj_x[step - 1])

    def proj_rows(step):
        return proj.at[col, pl.ds(place.along_z(step) * ring, ring)]

    proj_z = [mail.push(proj_rows(0), proj_rows(0), place.to_z(step)) for step in range(1, ring)]
    text_z = [mail.push(own_text, own_text, place.to_z(step)) for step in (1, 3, 2)]
    raw_student = jnp.dot(si_ref[...], sp_ref[...], preferred_element_type=jnp.float32)
    raw_ref[...] = raw_student
    img_s_ref[col] = unit_rows(raw_student).astype(jnp.bfloat16)
    student = AlongColumn(mail, place, img_s_ref)
    student.start()
    own_pairs = pairs_ref.at[col]
    pair_mail = [
        mail.push(own_pairs, own_pairs, {"col": (col + step) % n_col}) for step in range(1, n_col)
    ]
    for step in range(1, n_row):
        mail.got(orders.at[(row + n_row - step) % n_row], order_mail[step - 1])
    lanes = lax.broadcasted_iota(jnp.int32, (per_device, 2 * per_device), 1).astype(jnp.float32)

    def pick(target, carry):
        wanted = (orders[target] - col * (n_row * per_device)).astype(jnp.float32)
        wanted = jnp.broadcast_to(wanted, (per_device, per_device)).T
        wanted = jnp.concatenate([wanted, wanted], axis=1)
        total = jnp.zeros((per_device, ti_ref.shape[1]), jnp.float32)
        for start in range(0, n_row * per_device, 2 * per_device):
            chosen = jnp.where(wanted == lanes + float(start), 1.0, 0.0).astype(jnp.bfloat16)
            total += jnp.dot(
                chosen,
                ti_ref[start : start + 2 * per_device],
                preferred_element_type=jnp.float32,
            )
        feat_out[target] = total.astype(jnp.bfloat16)
        return carry

    lax.fori_loop(0, n_row, pick, 0)
    feat_mail = []
    for step in range(1, n_row):
        target = (row + step) % n_row
        feat_mail.append(mail.push(feat_out.at[target], feat_in.at[row], {"row": target}))
    feat_in[row] = feat_out[row]
    for step in range(1, ring):
        mail.got(proj_rows(-step), proj_z[step - 1])
    gathered_proj = AlongColumn(mail, place, proj)
    gathered_proj.start()
    student.forward()
    mail.got(block(-1, 0), text_z[0])
    spread(-1)
    mail.got(block(1, 0), text_z[1])
    spread(1)
    mail.got(block(2, 0), text_z[2])
    spread(2)
    gathered_proj.forward()
    student.last()
    right_half, left_half = {}, {}

    def pass_on(step):
        mail.got(block(step, -1), right[step])
        right_half[step] = mail.push(part(step, -1, 0), part(step, -1, 0), place.to_x(1))
        mail.got(block(step, 1), left[step])
        left_half[step] = mail.push(part(step, 1, 1), part(step, 1, 1), place.to_x(-1))

    pass_on(0)
    gathered_proj.last()
    gathered_proj.end()
    for step in range(1, n_row):
        mail.got(feat_in.at[(row + n_row - step) % n_row], feat_mail[step - 1])
    width = pt_ref.shape[0]

    def project(source, carry):
        total = jnp.zeros((width, per_device), jnp.float32)
        for features in range(n_row):
            total += lax.dot_general(
                proj[source, features],
                feat_in[features],
                nt_dims,
                preferred_element_type=jnp.float32,
            )
        embed[pl.ds(pl.multiple_of(source * width, 8), width), :] = total
        return carry

    lax.fori_loop(0, n_col, project, 0)
    raw_teacher = embed[...]
    scale = lax.rsqrt(jnp.sum(raw_teacher * raw_teacher, axis=0, keepdims=True) + norm_eps)
    img_t_ref[col] = (raw_teacher * scale).T.astype(jnp.bfloat16)
    teacher = AlongColumn(mail, place, img_t_ref)
    teacher.start()
    student.end()
    pass_on(-1)
    teacher.forward()
    pass_on(1)
    teacher.last()
    pass_on(2)
    for step in (0, -1, 1, 2):
        mail.got(part(step, 2, 0), right_half[step])
        mail.got(part(step, 2, 1), left_half[step])
    teacher.end()
    for step in range(1, n_col):
        mail.got(pairs_ref.at[(col + n_col - step) % n_col], pair_mail[step - 1])
    mail.finish()


def vmem():
    return pl.BlockSpec(memory_space=pltpu.VMEM)


def gather_tiles(si, sp, st, ti, pt, tt, order, pair):
    per_device = st.shape[0]
    width = st.shape[1]
    teacher_width = tt.shape[1]
    features = ti.shape[1]
    bf16, f32 = jnp.bfloat16, jnp.float32
    return pl.pallas_call(
        gather_kernel,
        out_shape=(
            jax.ShapeDtypeStruct((n_row, per_device, teacher_width + width), bf16),
            jax.ShapeDtypeStruct((n_col, per_device, width), bf16),
            jax.ShapeDtypeStruct((n_col, per_device, teacher_width), bf16),
            jax.ShapeDtypeStruct((n_col, 1, per_device), jnp.int32),
            jax.ShapeDtypeStruct((per_device, width), f32),
        ),
        in_specs=[vmem()] * 8,
        out_specs=[vmem()] * 5,
        scratch_shapes=[
            pltpu.VMEM((n_row, 1, per_device), jnp.int32),
            pltpu.VMEM((n_row, per_device, features), bf16),
            pltpu.VMEM((n_row, per_device, features), bf16),
            pltpu.VMEM((n_col, n_row, pt.shape[0], features), bf16),
            pltpu.VMEM((teacher_width, per_device), f32),
            pltpu.SemaphoreType.DMA((128,)),
            pltpu.SemaphoreType.DMA((128,)),
        ],
        compiler_params=pltpu.CompilerParams(
            collective_id=0, has_side_effects=True, vmem_limit_bytes=48 * 1024 * 1024
        ),
    )(si, sp, st, ti, pt, tt, order, pair)


def stats_kernel(rows_ref, cols_ref, rows_out, cols_out, rows_in, cols_in, send_sem, recv_sem):
    place = Place()
    mail = Mail(send_sem, recv_sem)
    greet(all_peers(place))
    sides = (
        ("row", place.row, n_row, cols_ref, cols_in, cols_out),
        ("col", place.col, n_col, rows_ref, rows_in, rows_out),
    )
    tickets = []
    for axis, own, size, source, landed, _ in sides:
        tickets.append(
            [
                mail.push(
                    source.at[(own + step) % size],
                    landed.at[own],
                    {axis: (own + step) % size},
                )
                for step in range(1, size)
            ]
        )
        landed[own] = source[own]
    back = []
    for (axis, own, size, source, landed, out), waits in zip(sides, tickets):
        for step in range(1, size):
            mail.got(landed.at[(own + size - step) % size], waits[step - 1])
        parts = landed[...]
        lse = []
        for kind in range(2):
            highest = jnp.max(parts[:, 2 * kind], axis=0, keepdims=True)
            total = jnp.sum(
                parts[:, 2 * kind + 1] * jnp.exp(parts[:, 2 * kind] - highest),
                axis=0,
                keepdims=True,
            )
            lse.append(highest + jnp.log(total))
        rest = jnp.zeros((6, lse[0].shape[1]), jnp.float32)
        out[own] = jnp.concatenate(lse + [rest], axis=0)
        back.append(
            [
                mail.push(out.at[own], out.at[own], {axis: (own + step) % size})
                for step in range(1, size)
            ]
        )
    for (axis, own, size, source, landed, out), waits in zip(sides, back):
        for step in range(1, size):
            mail.got(out.at[(own + size - step) % size], waits[step - 1])
    mail.finish()


def exchange_stats(rows, cols):
    shapes = [jax.ShapeDtypeStruct(a.shape, jnp.float32) for a in (rows, cols)]
    return pl.pallas_call(
        stats_kernel,
        out_shape=tuple(shapes),
        in_specs=[vmem()] * 2,
        out_specs=[vmem()] * 2,
        scratch_shapes=[
            pltpu.VMEM(rows.shape, jnp.float32),
            pltpu.VMEM(cols.shape, jnp.float32),
            pltpu.SemaphoreType.DMA((64,)),
            pltpu.SemaphoreType.DMA((64,)),
        ],
        compiler_params=pltpu.CompilerParams(collective_id=1, has_side_effects=True),
    )(rows, cols)


def tail_kernel(
    part_ref,
    si_ref,
    raw_ref,
    embed_out,
    proj_out,
    from_core,
    leaving,
    arriving,
    partial,
    from_sibling,
    summed,
    first_in,
    second,
    second_in,
    third,
    third_in,
    fourth,
    fourth_in,
    send_sem,
    recv_sem,
):
    place = Place()
    mail = Mail(send_sem, recv_sem)
    core, y = place.core, place.y
    other = 1 - core
    greet(
        [place.sibling(), {"group": 1 - lax.axis_index("group")}]
        + [place.to_x(step) for step in range(1, ring)]
        + [place.to_y(step) for step in range(1, ring)]
        + [place.to_z(step) for step in range(1, ring)]
    )
    over = []
    for step in (1, 3, 2, 0):
        target = place.along_y(step)
        over.append(
            (
                step,
                mail.push(part_ref.at[target * 2 + other], from_core.at[target], place.sibling()),
            )
        )
    across = []
    for step, ticket in over:
        target = place.along_y(step)
        mail.got(from_core.at[target], ticket)
        total = part_ref[target * 2 + core] + from_core[target]
        if step:
            leaving[step - 1] = total.astype(jnp.bfloat16)
            across.append(
                (
                    step,
                    mail.push(
                        leaving.at[step - 1], arriving.at[step - 1], place.to_y(step)
                    ),
                )
            )
    embed_grad = total
    for step, ticket in across:
        mail.got(arriving.at[step - 1], ticket)
        embed_grad = embed_grad + arriving[step - 1].astype(jnp.float32)
    embed_grad = logit_scale * embed_grad
    raw_student = raw_ref[...]
    scale = lax.rsqrt(jnp.sum(raw_student * raw_student, axis=1, keepdims=True) + norm_eps)
    student_unit = raw_student * scale
    inner_term = jnp.sum(student_unit * embed_grad, axis=1, keepdims=True)
    grad_embed = (embed_grad - student_unit * inner_term) * scale
    embed_out[...] = grad_embed
    rounded = grad_embed.astype(jnp.bfloat16)
    parts, lanes, size = partial.shape[1], partial.shape[2], partial.shape[3]
    for half in range(2):
        for kind in range(parts):
            start = (half * parts + kind) * size
            product = lax.dot_general(
                si_ref[:, start : start + size],
                rounded,
                tn_dims,
                preferred_element_type=jnp.float32,
            )
            for lane in range(lanes):
                partial[half, kind, lane] = product[:, lane * size : (lane + 1) * size]
    ticket = mail.push(partial.at[other], from_sibling, place.sibling())
    mail.got(from_sibling, ticket)
    summed[...] = partial[core] + from_sibling[...]
    along = {
        "x": (place.x, place.along_x, place.to_x),
        "y": (place.y, place.along_y, place.to_y),
        "z": (place.z, place.along_z, place.to_z),
    }
    orders = ("yxz", "xzy", "zyx")

    def rows_of(position, count):
        return pl.ds(pl.multiple_of(position * count, 8), count)

    tickets = {}
    for kind in range(parts):
        own, at, to = along[orders[kind][0]]
        for step in range(1, ring):
            tickets[kind, step] = mail.push(
                summed.at[kind, at(step)], first_in.at[kind, step - 1], to(step)
            )
    for kind in range(parts):
        own, at, to = along[orders[kind][0]]
        total = summed[kind, own]
        for step in range(1, ring):
            mail.got(first_in.at[kind, step - 1], tickets[kind, step])
            total = total + first_in[kind, step - 1]
        second[kind] = total
        own, at, to = along[orders[kind][1]]
        for step in range(1, ring):
            tickets[kind, step] = mail.push(
                second.at[kind, rows_of(at(step), 32)], second_in.at[kind, step - 1], to(step)
            )
    for kind in range(parts):
        own, at, to = along[orders[kind][1]]
        total = second[kind, rows_of(own, 32)]
        for step in range(1, ring):
            mail.got(second_in.at[kind, step - 1], tickets[kind, step])
            total = total + second_in[kind, step - 1]
        third[kind] = total
        own, at, to = along[orders[kind][2]]
        for step in range(1, ring):
            tickets[kind, step] = mail.push(
                third.at[kind, rows_of(at(step), 8)], third_in.at[kind, step - 1], to(step)
            )
    for kind in range(parts):
        own, at, to = along[orders[kind][2]]
        total = third[kind, rows_of(own, 8)]
        for step in range(1, ring):
            mail.got(third_in.at[kind, step - 1], tickets[kind, step])
            total = total + third_in[kind, step - 1]
        fourth[kind] = total
        tickets[kind, 0] = mail.push(
            fourth.at[kind], fourth_in.at[kind], {"group": 1 - lax.axis_index("group")}
        )

    def piece(kind, level, step):
        own1, at1, to1 = along[orders[kind][0]]
        own2, at2, to2 = along[orders[kind][1]]
        own3, at3, to3 = along[orders[kind][2]]
        if level == 3:
            start = own2 * 32 + at3(step) * 8
            return proj_out.at[core, kind, own1, pl.ds(pl.multiple_of(start, 8), 8)]
        if level == 2:
            return proj_out.at[core, kind, own1, rows_of(at2(step), 32)]
        return proj_out.at[core, kind, at1(step)]

    def send_piece(kind, level):
        to = along[orders[kind][level - 1]][2]
        for step in range(1, ring):
            tickets[kind, step] = mail.push(
                piece(kind, level, 0), piece(kind, level, 0), to(step)
            )

    def land_piece(kind, level):
        for step in range(1, ring):
            mail.got(piece(kind, level, -step), tickets[kind, step])

    for kind in range(parts):
        mail.got(fourth_in.at[kind], tickets[kind, 0])
        piece(kind, 3, 0)[...] = fourth[kind] + fourth_in[kind]
        send_piece(kind, 3)
    for level in (3, 2):
        for kind in range(parts):
            land_piece(kind, level)
            send_piece(kind, level - 1)
    for kind in range(parts):
        land_piece(kind, 1)
    ticket = mail.push(proj_out.at[core], proj_out.at[core], place.sibling())
    mail.got(proj_out.at[other], ticket)
    mail.finish()


def finish_grads(partial, si, raw_student):
    per_device, width = raw_student.shape
    size = 128
    parts = si.shape[1] // (2 * size)
    lanes = width // size
    f32 = jnp.float32
    return pl.pallas_call(
        tail_kernel,
        out_shape=(
            jax.ShapeDtypeStruct((per_device, width), f32),
            jax.ShapeDtypeStruct((2, parts, lanes, size, size), f32),
        ),
        in_specs=[vmem()] * 3,
        out_specs=[vmem()] * 2,
        scratch_shapes=[
            pltpu.VMEM((ring, per_device, width), f32),
            pltpu.VMEM((ring - 1, per_device, width), jnp.bfloat16),
            pltpu.VMEM((ring - 1, per_device, width), jnp.bfloat16),
            pltpu.VMEM((2, parts, lanes, size, size), f32),
            pltpu.VMEM((parts, lanes, size, size), f32),
            pltpu.VMEM((parts, lanes, size, size), f32),
            pltpu.VMEM((parts, ring - 1, size, size), f32),
            pltpu.VMEM((parts, size, size), f32),
            pltpu.VMEM((parts, ring - 1, size // 4, size), f32),
            pltpu.VMEM((parts, size // 4, size), f32),
            pltpu.VMEM((parts, ring - 1, 8, size), f32),
            pltpu.VMEM((parts, 8, size), f32),
            pltpu.VMEM((parts, 8, size), f32),
            pltpu.SemaphoreType.DMA((80,)),
            pltpu.SemaphoreType.DMA((80,)),
        ],
        compiler_params=pltpu.CompilerParams(
            collective_id=2, has_side_effects=True, vmem_limit_bytes=40 * 1024 * 1024
        ),
    )(partial, si, raw_student)


def body(
    student_image,
    student_proj,
    student_text,
    teacher_image,
    teacher_proj,
    teacher_text,
    assignment,
    pair_ids,
):
    per_device = student_image.shape[0]
    width = student_proj.shape[1]
    teacher_width = teacher_text.shape[1]
    text, image_student, image_teacher, image_pairs, raw_student = gather_tiles(
        student_image,
        student_proj,
        student_text,
        teacher_image,
        teacher_proj.T,
        teacher_text,
        assignment,
        pair_ids,
    )
    text = text.reshape(n_row * per_device, -1)
    text_teacher, text_student = text[:, :teacher_width], text[:, teacher_width:]
    image_student = image_student.reshape(n_col * per_device, -1)
    image_teacher = image_teacher.reshape(n_col * per_device, -1)
    image_pairs = image_pairs.reshape(-1)
    text_slots = jnp.arange(text_student.shape[0], dtype=jnp.int32)
    text_ids = (
        text_slots // per_device * n_col + lax.axis_index("col")
    ) * per_device + text_slots % per_device
    tile_rows = image_student.shape[0]
    block_rows = math.gcd(tile_rows, 512)
    block_starts = list(range(0, tile_rows, block_rows))
    teacher_blocks = []
    row_parts = []
    column_stats = None
    for start in block_starts:
        student_scores = tile_scores(image_student[start : start + block_rows], text_student)
        teacher_scores = tile_scores(image_teacher[start : start + block_rows], text_teacher)
        teacher_blocks.append(teacher_scores)
        row_parts.append(row_partial(student_scores) + row_partial(teacher_scores))
        block_columns = column_partial(student_scores) + column_partial(teacher_scores)
        column_stats = (
            block_columns if column_stats is None else merge_stats(column_stats, block_columns)
        )
    row_local = [
        jnp.concatenate([partial_stats[position] for partial_stats in row_parts])
        for position in range(4)
    ]

    def owners(values, size):
        stacked = jnp.stack(list(values) + [jnp.zeros_like(values[0])] * 4)
        return stacked.reshape(8, size, per_device).transpose(1, 0, 2)

    row_lse, col_lse = exchange_stats(owners(row_local, n_col), owners(column_stats, n_row))
    student_row, teacher_row = row_lse[:, 0].reshape(-1), row_lse[:, 1].reshape(-1)
    student_col, teacher_col = col_lse[:, 0].reshape(-1), col_lse[:, 1].reshape(-1)
    groups = lax.axis_size("group")
    partial_grads = []
    for position, start in enumerate(block_starts):
        student_scores = tile_scores(image_student[start : start + block_rows], text_student)
        teacher_scores = teacher_blocks[position]
        srow = student_row[start : start + block_rows]
        trow = teacher_row[start : start + block_rows]
        matched = (image_pairs[start : start + block_rows][:, None] == text_ids[None, :]).astype(
            jnp.float32
        )
        weights = (
            2.0 * jnp.exp(student_scores - srow[:, None])
            + 2.0 * jnp.exp(student_scores - student_col[None, :])
            - jnp.exp(teacher_scores - trow[:, None])
            - jnp.exp(teacher_scores - teacher_col[None, :])
            - 2.0 * matched
        ) / groups
        partial_grads.append(
            jnp.dot(weights.astype(jnp.bfloat16), text_student, preferred_element_type=jnp.float32)
        )
    partial = jnp.concatenate(partial_grads, 0).reshape(n_col, per_device, width)
    grad_embed, grad_proj = finish_grads(partial, student_image, raw_student)
    grad_proj = grad_proj.transpose(0, 1, 3, 2, 4).reshape(student_image.shape[1], width)
    return (grad_embed, grad_proj)


def solution(mesh):
    placed = (
        P(("group", "row", "col"), None),
        P(),
        P(("group", "row", "col"), None),
        P(("group", "col"), "row"),
        P("row", "col"),
        P(("group", "row", "col"), None),
        P("group", ("row", "col")),
        P("group", ("row", "col")),
    )
    return jax.shard_map(
        body,
        mesh=mesh,
        in_specs=placed,
        out_specs=(P(("group", "row", "col"), None), P()),
        check_vma=False,
    )
```

```python
import math

import jax
import jax.numpy as jnp
from jax import lax
from jax.experimental import pallas as pl
from jax.experimental.pallas import tpu as pltpu
from jax.sharding import PartitionSpec as P

logit_scale = 100.0
score_scale = logit_scale * math.log2(math.e)
lowest = -1e30
norm_eps = 1e-06
MESH = pl.DeviceIdType.MESH
ring = 4
n_row = 16
n_col = 8
nt_dims = (((1,), (1,)), ((), ()))
tn_dims = (((0,), (0,)), ((), ()))


def unit_rows(values):
    return values * lax.rsqrt(jnp.sum(values * values, axis=1, keepdims=True) + norm_eps)


class Place:
    def __init__(self):
        self.row = lax.axis_index("row")
        self.col = lax.axis_index("col")
        self.z, self.x = self.row // ring, self.row % ring
        self.y, self.core = self.col // 2, self.col % 2

    def along_x(self, step):
        return (self.x + step + ring) % ring

    def along_y(self, step):
        return (self.y + step + ring) % ring

    def along_z(self, step):
        return (self.z + step + ring) % ring

    def to_x(self, step):
        return {"row": self.z * ring + self.along_x(step)}

    def to_z(self, step):
        return {"row": self.along_z(step) * ring + self.x}

    def to_y(self, step):
        return {"col": self.along_y(step) * 2 + self.core}

    def sibling(self):
        return {"col": self.y * 2 + 1 - self.core}


class Mail:
    def __init__(self, send_sem, recv_sem):
        self.send_sem, self.recv_sem = send_sem, recv_sem
        self.used = 0
        self.sent = []

    def push(self, src, dst, device):
        index = self.used
        self.used += 1
        copy = pltpu.make_async_remote_copy(
            src_ref=src,
            dst_ref=dst,
            send_sem=self.send_sem.at[index],
            recv_sem=self.recv_sem.at[index],
            device_id=device,
            device_id_type=MESH,
        )
        copy.start()
        self.sent.append(copy)
        return index, device

    def got(self, slot, ticket):
        index, device = ticket
        pltpu.make_async_remote_copy(
            src_ref=slot,
            dst_ref=slot,
            send_sem=self.send_sem.at[index],
            recv_sem=self.recv_sem.at[index],
            device_id=device,
            device_id_type=MESH,
        ).wait_recv()

    def finish(self):
        for copy in self.sent:
            copy.wait_send()


def all_peers(place):
    return (
        [{"row": (place.row + step) % n_row} for step in range(1, n_row)]
        + [{"col": (place.col + step) % n_col} for step in range(1, n_col)]
        + [{"group": 1 - lax.axis_index("group")}]
    )


class AlongColumn:
    def __init__(self, mail, place, ref):
        self.mail, self.place, self.ref = mail, place, ref
        self.half = ref.shape[1] // 2

    def block(self, step, core):
        return self.place.along_y(step) * 2 + core

    def lower(self, index):
        return self.ref.at[index, pl.ds(0, self.half)]

    def upper(self, index):
        return self.ref.at[index, pl.ds(self.half, self.half)]

    def start(self):
        place, mail = self.place, self.mail
        own = self.ref.at[place.col]
        self.up = mail.push(own, own, place.to_y(1))
        self.down = mail.push(own, own, place.to_y(-1))
        self.over = [mail.push(own, own, place.sibling())]

    def forward(self):
        place, mail = self.place, self.mail
        below = self.block(-1, place.core)
        mail.got(self.ref.at[below], self.up)
        self.up_half = mail.push(self.lower(below), self.lower(below), place.to_y(1))
        self.over.append(mail.push(self.ref.at[below], self.ref.at[below], place.sibling()))
        above = self.block(1, place.core)
        mail.got(self.ref.at[above], self.down)
        self.down_half = mail.push(self.upper(above), self.upper(above), place.to_y(-1))
        self.over.append(mail.push(self.ref.at[above], self.ref.at[above], place.sibling()))

    def last(self):
        place, mail = self.place, self.mail
        far = self.block(2, place.core)
        mail.got(self.lower(far), self.up_half)
        self.over.append(mail.push(self.lower(far), self.lower(far), place.sibling()))
        mail.got(self.upper(far), self.down_half)
        self.over.append(mail.push(self.upper(far), self.upper(far), place.sibling()))

    def end(self):
        place, mail = self.place, self.mail
        other = 1 - place.core
        mail.got(self.ref.at[self.block(0, other)], self.over[0])
        mail.got(self.ref.at[self.block(-1, other)], self.over[1])
        mail.got(self.ref.at[self.block(1, other)], self.over[2])
        far = self.block(2, other)
        mail.got(self.lower(far), self.over[3])
        mail.got(self.upper(far), self.over[4])


def step_kernel(
    si_hbm,
    sp_hbm,
    st_hbm,
    ti_hbm,
    pt_hbm,
    tt_hbm,
    order_hbm,
    pair_hbm,
    embed_out,
    proj_out,
    si_ref,
    sp_ref,
    st_ref,
    ti_ref,
    tt_ref,
    text,
    img_s,
    img_t,
    pairs,
    raw_ref,
    orders,
    feat_out,
    feat_in,
    proj,
    embed,
    scores,
    row_high,
    row_total,
    col_high,
    col_total,
    row_stats,
    row_landed,
    row_lse,
    col_stats,
    col_landed,
    col_lse,
    row_tiles,
    offsets,
    partial_grad,
    from_core,
    leaving,
    arriving,
    partial,
    from_sibling,
    summed,
    first_in,
    second,
    second_in,
    third,
    third_in,
    fourth,
    fourth_in,
    load_sem,
    send_sem,
    recv_sem,
):
    place = Place()
    mail = Mail(send_sem, recv_sem)
    row, col, core = place.row, place.col, place.core
    other = 1 - core
    per_device, width = st_ref.shape
    teacher_width = tt_ref.shape[1]
    half = per_device // 2

    loads = []
    for source, target in (
        (order_hbm, orders.at[row]),
        (pt_hbm, proj.at[col, row]),
        (pair_hbm, pairs.at[col]),
        (st_hbm, st_ref),
        (tt_hbm, tt_ref),
        (si_hbm, si_ref),
        (sp_hbm, sp_ref),
        (ti_hbm, ti_ref),
    ):
        copy = pltpu.make_async_copy(source, target, load_sem.at[len(loads)])
        copy.start()
        loads.append(copy)
    barrier = pltpu.get_barrier_semaphore()
    peers = all_peers(place)
    for device in peers:
        pl.semaphore_signal(barrier, inc=1, device_id=device, device_id_type=MESH)
    for copy in loads[:5]:
        copy.wait()
    own_x, own_z = place.x, place.z
    text[own_x, own_z, :, :teacher_width] = unit_rows(tt_ref[...].astype(jnp.float32)).astype(
        jnp.bfloat16
    )
    text[own_x, own_z, :, teacher_width:] = unit_rows(st_ref[...].astype(jnp.float32)).astype(
        jnp.bfloat16
    )
    pl.semaphore_wait(barrier, len(peers))

    own_order = orders.at[row]
    order_mail = [
        mail.push(own_order, own_order, {"row": (row + step) % n_row}) for step in range(1, n_row)
    ]
    own_proj = proj.at[col, row]
    proj_x = [mail.push(own_proj, own_proj, place.to_x(step)) for step in (1, 3, 2)]

    def block(dx, dz, part):
        return text.at[place.along_x(dx), place.along_z(dz), pl.ds(part * half, half)]

    z_up, z_down, x_up, x_down, x_on = {}, {}, {}, {}, {}

    def start_z(part):
        z_up[part] = mail.push(block(0, 0, part), block(0, 0, part), place.to_z(1))
        z_down[part] = mail.push(block(0, 0, part), block(0, 0, part), place.to_z(-1))

    def start_x(dz, part):
        x_up[dz, part] = mail.push(block(0, dz, part), block(0, dz, part), place.to_x(1))
        x_down[dz, part] = mail.push(block(0, dz, part), block(0, dz, part), place.to_x(-1))

    def forward_x(dz):
        mail.got(block(-1, dz, 0), x_up[dz, 0])
        x_on[dz, 0] = mail.push(block(-1, dz, 0), block(-1, dz, 0), place.to_x(1))
        mail.got(block(1, dz, 1), x_down[dz, 1])
        x_on[dz, 1] = mail.push(block(1, dz, 1), block(1, dz, 1), place.to_x(-1))

    start_z(0)
    start_x(0, 0)
    start_x(0, 1)
    loads[5].wait()
    loads[6].wait()
    raw_student = jnp.dot(si_ref[...], sp_ref[...], preferred_element_type=jnp.float32)
    raw_ref[...] = raw_student
    img_s[col] = unit_rows(raw_student).astype(jnp.bfloat16)
    student = AlongColumn(mail, place, img_s)
    student.start()
    own_pairs = pairs.at[col]
    pair_mail = [
        mail.push(own_pairs, own_pairs, {"col": (col + step) % n_col}) for step in range(1, n_col)
    ]
    for step, ticket in zip((1, 3, 2), proj_x):
        mail.got(proj.at[col, place.z * ring + place.along_x(-step)], ticket)

    def proj_rows(step):
        return proj.at[col, pl.ds(place.along_z(step) * ring, ring)]

    proj_z = [mail.push(proj_rows(0), proj_rows(0), place.to_z(step)) for step in (1, 3, 2)]
    start_z(1)

    loads[7].wait()
    for step in range(1, n_row):
        mail.got(orders.at[(row + n_row - step) % n_row], order_mail[step - 1])
    lanes = lax.broadcasted_iota(jnp.int32, (per_device, 2 * per_device), 1).astype(jnp.float32)

    def pick(target, carry):
        wanted = (orders[target] - col * (n_row * per_device)).astype(jnp.float32)
        wanted = jnp.broadcast_to(wanted, (per_device, per_device)).T
        wanted = jnp.concatenate([wanted, wanted], axis=1)
        total = jnp.zeros((per_device, ti_ref.shape[0]), jnp.float32)
        for start in range(0, n_row * per_device, 2 * per_device):
            chosen = jnp.where(wanted == lanes + float(start), 1.0, 0.0).astype(jnp.bfloat16)
            total += lax.dot_general(
                chosen,
                ti_ref[:, start : start + 2 * per_device],
                nt_dims,
                preferred_element_type=jnp.float32,
            )
        feat_out[target] = total.astype(jnp.bfloat16)
        return carry

    lax.fori_loop(0, n_row, pick, 0)
    feat_mail = []
    for step in range(1, n_row):
        target = (row + step) % n_row
        feat_mail.append(mail.push(feat_out.at[target], feat_in.at[row], {"row": target}))
    feat_in[row] = feat_out[row]

    mail.got(block(0, -1, 0), z_up[0])
    z_up_on = mail.push(block(0, -1, 0), block(0, -1, 0), place.to_z(1))
    start_x(-1, 0)
    mail.got(block(0, 1, 0), z_down[0])
    start_x(1, 0)
    student.forward()
    forward_x(0)
    for step, ticket in zip((1, 3, 2), proj_z):
        mail.got(proj_rows(-step), ticket)
    gathered_proj = AlongColumn(mail, place, proj)
    gathered_proj.start()
    mail.got(block(0, 1, 1), z_down[1])
    z_down_on = mail.push(block(0, 1, 1), block(0, 1, 1), place.to_z(-1))
    start_x(1, 1)
    mail.got(block(0, -1, 1), z_up[1])
    start_x(-1, 1)
    student.last()
    gathered_proj.forward()
    mail.got(block(0, 2, 0), z_up_on)
    start_x(2, 0)
    mail.got(block(0, 2, 1), z_down_on)
    start_x(2, 1)
    gathered_proj.last()
    gathered_proj.end()
    for step in range(1, n_row):
        mail.got(feat_in.at[(row + n_row - step) % n_row], feat_mail[step - 1])
    proj_width = proj.shape[2]

    def project(source, carry):
        total = jnp.zeros((proj_width, per_device), jnp.float32)
        for features in range(n_row):
            total += lax.dot_general(
                proj[source, features],
                feat_in[features],
                nt_dims,
                preferred_element_type=jnp.float32,
            )
        embed[pl.ds(pl.multiple_of(source * proj_width, 8), proj_width), :] = total
        return carry

    lax.fori_loop(0, n_col, project, 0)
    raw_teacher = embed[...]
    scale = lax.rsqrt(jnp.sum(raw_teacher * raw_teacher, axis=0, keepdims=True) + norm_eps)
    img_t[col] = (raw_teacher * scale).T.astype(jnp.bfloat16)
    teacher = AlongColumn(mail, place, img_t)
    teacher.start()
    student.end()
    forward_x(-1)
    teacher.forward()
    forward_x(1)
    teacher.last()
    for step in range(1, n_col):
        mail.got(pairs.at[(col + n_col - step) % n_col], pair_mail[step - 1])
    slot = lax.broadcasted_iota(jnp.int32, (per_device, per_device), 1)
    for source in range(n_col):
        wide = jnp.broadcast_to(pairs[source].astype(jnp.float32), (per_device, per_device)).T
        offsets[source * per_device : (source + 1) * per_device] = wide.astype(jnp.int32) - slot
    row_high[...] = jnp.full(row_high.shape, lowest, jnp.float32)
    row_total[...] = jnp.zeros(row_total.shape, jnp.float32)
    teacher.end()

    image_rows = 2 * per_device
    chunk = ring * per_device
    col_mail = {}

    def text_student(index):
        return text[index, :, :, teacher_width:].reshape(chunk, width)

    def text_teacher(index):
        return text[index, :, :, :teacher_width].reshape(chunk, teacher_width)

    def process(dx):
        index = place.along_x(dx)
        col_high[...] = jnp.full(col_high.shape, lowest, jnp.float32)
        col_total[...] = jnp.zeros(col_total.shape, jnp.float32)

        def images(step, carry):
            rows = pl.ds(pl.multiple_of(step * image_rows, image_rows), image_rows)
            for kind in range(2):
                if kind == 0:
                    left = img_s[pl.ds(2 * step, 2)].reshape(image_rows, width)
                    right = text_student(index)
                else:
                    left = img_t[pl.ds(2 * step, 2)].reshape(image_rows, teacher_width)
                    right = text_teacher(index)
                values = score_scale * lax.dot_general(
                    left, right, nt_dims, preferred_element_type=jnp.float32
                )
                scores[kind, index, rows] = values
                tiles = [
                    values[:, start : start + per_device] for start in range(0, chunk, per_device)
                ]
                before = row_high[kind, rows]
                high = before
                for tile in tiles:
                    high = jnp.maximum(high, tile)
                total = row_total[kind, rows] * jnp.exp2(before - high)
                for tile in tiles:
                    total = total + jnp.exp2(tile - high)
                row_high[kind, rows] = high
                row_total[kind, rows] = total
                stacked = values.reshape(image_rows // 8, 8, chunk)
                before = col_high[kind]
                high = jnp.maximum(before, jnp.max(stacked, axis=0))
                total = col_total[kind] * jnp.exp2(before - high)
                col_total[kind] = total + jnp.sum(jnp.exp2(stacked - high[None]), axis=0)
                col_high[kind] = high
            return carry

        lax.fori_loop(0, ring, images, 0)
        found = []
        for kind in range(2):
            high = jnp.max(col_high[kind], axis=0, keepdims=True)
            total = jnp.sum(
                col_total[kind] * jnp.exp2(col_high[kind] - high), axis=0, keepdims=True
            )
            found += [high, total]
        found = jnp.concatenate(found + [jnp.zeros((4, chunk), jnp.float32)], axis=0)
        for z in range(ring):
            col_stats[index, z] = found[:, z * per_device : (z + 1) * per_device]
        for dz in range(ring):
            z = place.along_z(dz)
            if dx or dz:
                col_mail[dx, dz] = mail.push(
                    col_stats.at[index, z],
                    col_landed.at[own_x, own_z],
                    {"row": z * ring + index},
                )
            else:
                col_landed[own_x, own_z] = col_stats[index, z]

    process(0)
    forward_x(2)
    for dx, part, tickets in ((-1, 1, x_up), (1, 0, x_down)):
        for dz in (0, -1, 1, 2):
            mail.got(block(dx, dz, part), tickets[dz, part])
        process(dx % ring)
    for part in range(2):
        for dz in (0, -1, 1, 2):
            mail.got(block(2, dz, part), x_on[dz, part])
    process(2)

    for source in range(n_col):
        rows = slice(source * per_device, (source + 1) * per_device)
        found = []
        for kind in range(2):
            high_all = row_high[kind, rows].T
            high = jnp.max(high_all, axis=0, keepdims=True)
            total = jnp.sum(
                row_total[kind, rows].T * jnp.exp2(high_all - high), axis=0, keepdims=True
            )
            found += [high, total]
        row_stats[source] = jnp.concatenate(
            found + [jnp.zeros((4, per_device), jnp.float32)], axis=0
        )
    row_mail = [
        mail.push(
            row_stats.at[(col + step) % n_col],
            row_landed.at[col],
            {"col": (col + step) % n_col},
        )
        for step in range(1, n_col)
    ]
    row_landed[col] = row_stats[col]

    def merge(parts):
        found = []
        for kind in range(2):
            high = jnp.max(parts[:, 2 * kind], axis=0, keepdims=True)
            total = jnp.sum(
                parts[:, 2 * kind + 1] * jnp.exp2(parts[:, 2 * kind] - high),
                axis=0,
                keepdims=True,
            )
            found.append(high + jnp.log2(total) + float(kind))
        return jnp.concatenate(found + [jnp.zeros((6, per_device), jnp.float32)], axis=0)

    pairs_of_steps = [(dx, dz) for dx in range(ring) for dz in range(ring) if dx or dz]
    for dx, dz in pairs_of_steps:
        mail.got(col_landed.at[place.along_x(-dx), place.along_z(-dz)], col_mail[dx, dz])
    col_lse[own_x, own_z] = merge(col_landed[...].reshape(n_row, 8, per_device))
    own_lse = col_lse.at[own_x, own_z]
    col_back = {
        (dx, dz): mail.push(
            own_lse, own_lse, {"row": place.along_z(dz) * ring + place.along_x(dx)}
        )
        for dx, dz in pairs_of_steps
    }
    for step in range(1, n_col):
        mail.got(row_landed.at[(col + n_col - step) % n_col], row_mail[step - 1])
    row_lse[col] = merge(row_landed[...])
    row_back = [
        mail.push(row_lse.at[col], row_lse.at[col], {"col": (col + step) % n_col})
        for step in range(1, n_col)
    ]
    for step in range(1, n_col):
        mail.got(row_lse.at[(col + n_col - step) % n_col], row_back[step - 1])
    for source in range(n_col):
        rows = slice(source * per_device, (source + 1) * per_device)
        for kind in range(2):
            wide = row_lse[source, kind : kind + 1, :]
            row_tiles[kind, rows] = jnp.broadcast_to(wide, (per_device, per_device)).T
    for dx, dz in pairs_of_steps:
        mail.got(col_lse.at[place.along_x(-dx), place.along_z(-dz)], col_back[dx, dz])

    over = {}
    across = {}

    def weigh(step):
        target = place.along_y(step)
        rows = pl.ds(pl.multiple_of(target * image_rows, image_rows), image_rows)
        partial_grad[target] = jnp.zeros(partial_grad.shape[1:], jnp.float32)

        def texts(index, carry):
            parts = []
            for z in range(ring):
                lane = slice(z * per_device, (z + 1) * per_device)
                student_scores = scores[0, index, rows, lane]
                teacher_scores = scores[1, index, rows, lane]
                first_id = ((z * ring + index) * n_col + col) * per_device
                matched = jnp.where(offsets[rows] == first_id, 1.0, 0.0)
                weights = (
                    jnp.exp2(student_scores - row_tiles[0, rows])
                    + jnp.exp2(student_scores - col_lse[index, z, 0:1, :])
                    - jnp.exp2(teacher_scores - row_tiles[1, rows])
                    - jnp.exp2(teacher_scores - col_lse[index, z, 1:2, :])
                    - matched
                )
                parts.append(weights.astype(jnp.bfloat16))
            product = jnp.dot(
                jnp.concatenate(parts, axis=1),
                text_student(index),
                preferred_element_type=jnp.float32,
            )
            partial_grad[target] += product.reshape(2, per_device, width)
            return carry

        lax.fori_loop(0, ring, texts, 0)
        over[step] = mail.push(
            partial_grad.at[target, other], from_core.at[target], place.sibling()
        )

    def pass_over(step):
        target = place.along_y(step)
        mail.got(from_core.at[target], over[step])
        total = partial_grad[target, core] + from_core[target]
        if step:
            leaving[step - 1] = total.astype(jnp.bfloat16)
            across[step] = mail.push(
                leaving.at[step - 1], arriving.at[step - 1], place.to_y(step)
            )
        return total

    weigh(2)
    weigh(1)
    pass_over(2)
    weigh(3)
    pass_over(1)
    weigh(0)
    pass_over(3)
    embed_grad = pass_over(0)
    for step in (2, 1, 3):
        mail.got(arriving.at[step - 1], across[step])
        embed_grad = embed_grad + arriving[step - 1].astype(jnp.float32)
    embed_grad = logit_scale * embed_grad
    raw_student = raw_ref[...]
    scale = lax.rsqrt(jnp.sum(raw_student * raw_student, axis=1, keepdims=True) + norm_eps)
    student_unit = raw_student * scale
    inner_term = jnp.sum(student_unit * embed_grad, axis=1, keepdims=True)
    grad_embed = (embed_grad - student_unit * inner_term) * scale
    embed_out[...] = grad_embed
    rounded = grad_embed.astype(jnp.bfloat16)

    kinds, pieces, size = partial.shape[1], partial.shape[2], partial.shape[3]
    for side in range(2):
        for kind in range(kinds):
            start = (side * kinds + kind) * size
            product = lax.dot_general(
                si_ref[:, start : start + size],
                rounded,
                tn_dims,
                preferred_element_type=jnp.float32,
            )
            for lane in range(pieces):
                partial[side, kind, lane] = product[:, lane * size : (lane + 1) * size]
    ticket = mail.push(partial.at[other], from_sibling, place.sibling())
    mail.got(from_sibling, ticket)
    summed[...] = partial[core] + from_sibling[...]
    along = {
        "x": (place.x, place.along_x, place.to_x),
        "y": (place.y, place.along_y, place.to_y),
        "z": (place.z, place.along_z, place.to_z),
    }
    axes = ("yxz", "xzy", "zyx")

    def rows_of(position, count):
        return pl.ds(pl.multiple_of(position * count, 8), count)

    tickets = {}
    for kind in range(kinds):
        own, at, to = along[axes[kind][0]]
        for step in range(1, ring):
            tickets[kind, step] = mail.push(
                summed.at[kind, at(step)], first_in.at[kind, step - 1], to(step)
            )
    for kind in range(kinds):
        own, at, to = along[axes[kind][0]]
        total = summed[kind, own]
        for step in range(1, ring):
            mail.got(first_in.at[kind, step - 1], tickets[kind, step])
            total = total + first_in[kind, step - 1]
        second[kind] = total
        own, at, to = along[axes[kind][1]]
        for step in range(1, ring):
            tickets[kind, step] = mail.push(
                second.at[kind, rows_of(at(step), 32)], second_in.at[kind, step - 1], to(step)
            )
    for kind in range(kinds):
        own, at, to = along[axes[kind][1]]
        total = second[kind, rows_of(own, 32)]
        for step in range(1, ring):
            mail.got(second_in.at[kind, step - 1], tickets[kind, step])
            total = total + second_in[kind, step - 1]
        third[kind] = total
        own, at, to = along[axes[kind][2]]
        for step in range(1, ring):
            tickets[kind, step] = mail.push(
                third.at[kind, rows_of(at(step), 8)], third_in.at[kind, step - 1], to(step)
            )
    for kind in range(kinds):
        own, at, to = along[axes[kind][2]]
        total = third[kind, rows_of(own, 8)]
        for step in range(1, ring):
            mail.got(third_in.at[kind, step - 1], tickets[kind, step])
            total = total + third_in[kind, step - 1]
        fourth[kind] = total
        tickets[kind, 0] = mail.push(
            fourth.at[kind], fourth_in.at[kind], {"group": 1 - lax.axis_index("group")}
        )

    def piece(kind, level, step):
        own1, at1, to1 = along[axes[kind][0]]
        own2, at2, to2 = along[axes[kind][1]]
        own3, at3, to3 = along[axes[kind][2]]
        if level == 3:
            start = own2 * 32 + at3(step) * 8
            return proj_out.at[core, kind, own1, pl.ds(pl.multiple_of(start, 8), 8)]
        if level == 2:
            return proj_out.at[core, kind, own1, rows_of(at2(step), 32)]
        return proj_out.at[core, kind, at1(step)]

    def send_piece(kind, level):
        to = along[axes[kind][level - 1]][2]
        for step in range(1, ring):
            tickets[kind, step] = mail.push(
                piece(kind, level, 0), piece(kind, level, 0), to(step)
            )

    def land_piece(kind, level):
        for step in range(1, ring):
            mail.got(piece(kind, level, -step), tickets[kind, step])

    for kind in range(kinds):
        mail.got(fourth_in.at[kind], tickets[kind, 0])
        piece(kind, 3, 0)[...] = fourth[kind] + fourth_in[kind]
        send_piece(kind, 3)
    for level in (3, 2):
        for kind in range(kinds):
            land_piece(kind, level)
            send_piece(kind, level - 1)
    for kind in range(kinds):
        land_piece(kind, 1)
    ticket = mail.push(proj_out.at[core], proj_out.at[core], place.sibling())
    mail.got(proj_out.at[other], ticket)
    mail.finish()


def body(
    student_image,
    student_proj,
    student_text,
    teacher_image,
    teacher_proj,
    teacher_text,
    assignment,
    pair_ids,
):
    per_device, width = student_text.shape
    teacher_width = teacher_text.shape[1]
    student_width = student_image.shape[1]
    features, proj_width = teacher_proj.shape
    size = 128
    kinds = student_width // (2 * size)
    pieces = width // size
    bf16, f32, i32 = jnp.bfloat16, jnp.float32, jnp.int32
    tile = (8, per_device)
    chunk = ring * per_device
    images = n_col * per_device
    hbm = pl.BlockSpec(memory_space=pl.ANY)
    vmem = pl.BlockSpec(memory_space=pltpu.VMEM)
    copies = 216
    grad_embed, grad_proj = pl.pallas_call(
        step_kernel,
        out_shape=(
            jax.ShapeDtypeStruct((per_device, width), f32),
            jax.ShapeDtypeStruct((2, kinds, pieces, size, size), f32),
        ),
        in_specs=[hbm] * 8,
        out_specs=[vmem] * 2,
        scratch_shapes=[
            pltpu.VMEM(student_image.shape, bf16),
            pltpu.VMEM(student_proj.shape, bf16),
            pltpu.VMEM(student_text.shape, bf16),
            pltpu.VMEM((features, n_row * per_device), bf16),
            pltpu.VMEM(teacher_text.shape, bf16),
            pltpu.VMEM((ring, ring, per_device, teacher_width + width), bf16),
            pltpu.VMEM((n_col, per_device, width), bf16),
            pltpu.VMEM((n_col, per_device, teacher_width), bf16),
            pltpu.VMEM((n_col, 1, per_device), i32),
            pltpu.VMEM((per_device, width), f32),
            pltpu.VMEM((n_row, 1, per_device), i32),
            pltpu.VMEM((n_row, per_device, features), bf16),
            pltpu.VMEM((n_row, per_device, features), bf16),
            pltpu.VMEM((n_col, n_row, proj_width, features), bf16),
            pltpu.VMEM((teacher_width, per_device), f32),
            pltpu.VMEM((2, ring, images, chunk), f32),
            pltpu.VMEM((2, images, per_device), f32),
            pltpu.VMEM((2, images, per_device), f32),
            pltpu.VMEM((2, 8, chunk), f32),
            pltpu.VMEM((2, 8, chunk), f32),
            pltpu.VMEM((n_col,) + tile, f32),
            pltpu.VMEM((n_col,) + tile, f32),
            pltpu.VMEM((n_col,) + tile, f32),
            pltpu.VMEM((ring, ring) + tile, f32),
            pltpu.VMEM((ring, ring) + tile, f32),
            pltpu.VMEM((ring, ring) + tile, f32),
            pltpu.VMEM((2, images, per_device), f32),
            pltpu.VMEM((images, per_device), i32),
            pltpu.VMEM((ring, 2, per_device, width), f32),
            pltpu.VMEM((ring, per_device, width), f32),
            pltpu.VMEM((ring - 1, per_device, width), bf16),
            pltpu.VMEM((ring - 1, per_device, width), bf16),
            pltpu.VMEM((2, kinds, pieces, size, size), f32),
            pltpu.VMEM((kinds, pieces, size, size), f32),
            pltpu.VMEM((kinds, pieces, size, size), f32),
            pltpu.VMEM((kinds, ring - 1, size, size), f32),
            pltpu.VMEM((kinds, size, size), f32),
            pltpu.VMEM((kinds, ring - 1, size // 4, size), f32),
            pltpu.VMEM((kinds, size // 4, size), f32),
            pltpu.VMEM((kinds, ring - 1, 8, size), f32),
            pltpu.VMEM((kinds, 8, size), f32),
            pltpu.VMEM((kinds, 8, size), f32),
            pltpu.SemaphoreType.DMA((8,)),
            pltpu.SemaphoreType.DMA((copies,)),
            pltpu.SemaphoreType.DMA((copies,)),
        ],
        compiler_params=pltpu.CompilerParams(
            collective_id=0, has_side_effects=True, vmem_limit_bytes=60 * 1024 * 1024
        ),
    )(
        student_image,
        student_proj,
        student_text,
        teacher_image.T,
        teacher_proj.T,
        teacher_text,
        assignment,
        pair_ids,
    )
    return grad_embed, grad_proj.transpose(0, 1, 3, 2, 4).reshape(student_width, width)


def solution(mesh):
    placed = (
        P(("group", "row", "col"), None),
        P(),
        P(("group", "row", "col"), None),
        P(("group", "col"), "row"),
        P("row", "col"),
        P(("group", "row", "col"), None),
        P("group", ("row", "col")),
        P("group", ("row", "col")),
    )
    return jax.shard_map(
        body,
        mesh=mesh,
        in_specs=placed,
        out_specs=(P(("group", "row", "col"), None), P()),
        check_vma=False,
    )
```

```python
import math

import jax
import jax.numpy as jnp
from jax import lax
from jax.experimental import pallas as pl
from jax.experimental.pallas import tpu as pltpu
from jax.sharding import PartitionSpec as P

logit_scale = 100.0
score_scale = logit_scale * math.log2(math.e)
lowest = -1e30
norm_eps = 1e-06
MESH = pl.DeviceIdType.MESH
ring = 4
n_row = 16
n_col = 8
nt_dims = (((1,), (1,)), ((), ()))
tn_dims = (((0,), (0,)), ((), ()))


def unit_rows(values):
    return values * lax.rsqrt(jnp.sum(values * values, axis=1, keepdims=True) + norm_eps)


class Place:
    def __init__(self):
        self.row = lax.axis_index("row")
        self.col = lax.axis_index("col")
        self.z, self.x = self.row // ring, self.row % ring
        self.y, self.core = self.col // 2, self.col % 2
        self.slot = self.x * 2 + self.core

    def along_x(self, step):
        return (self.x + step + ring) % ring

    def along_y(self, step):
        return (self.y + step + ring) % ring

    def along_z(self, step):
        return (self.z + step + ring) % ring

    def to_x(self, step):
        return {"row": self.z * ring + self.along_x(step)}

    def to_z(self, step):
        return {"row": self.along_z(step) * ring + self.x}

    def to_y(self, step):
        return {"col": self.along_y(step) * 2 + self.core}

    def to_slot(self, step):
        slot = (self.slot + step) % n_col
        return {"row": self.z * ring + slot // 2, "col": self.y * 2 + slot % 2}

    def to_text(self, dy, dz):
        return {
            "row": self.along_z(dz) * ring + self.x,
            "col": self.along_y(dy) * 2 + self.core,
        }

    def across(self, step):
        return {
            "group": 1 - lax.axis_index("group"),
            "row": self.along_z(step) * ring + self.x,
        }

    def sibling(self):
        return {"col": self.y * 2 + 1 - self.core}


class Mail:
    def __init__(self, send_sem, recv_sem):
        self.send_sem, self.recv_sem = send_sem, recv_sem
        self.used = 0
        self.sent = {}

    def push(self, src, dst, device):
        index = self.used
        self.used += 1
        turn = index % self.send_sem.shape[0]
        if turn in self.sent:
            self.sent[turn].wait_send()
        copy = pltpu.make_async_remote_copy(
            src_ref=src,
            dst_ref=dst,
            send_sem=self.send_sem.at[turn],
            recv_sem=self.recv_sem.at[index],
            device_id=device,
            device_id_type=MESH,
        )
        copy.start()
        self.sent[turn] = copy
        return index, device

    def got(self, slot, ticket):
        index, device = ticket
        pltpu.make_async_remote_copy(
            src_ref=slot,
            dst_ref=slot,
            send_sem=self.send_sem.at[0],
            recv_sem=self.recv_sem.at[index],
            device_id=device,
            device_id_type=MESH,
        ).wait_recv()

    def finish(self):
        for copy in self.sent.values():
            copy.wait_send()


def all_peers(place):
    return (
        [{"row": (place.row + step) % n_row} for step in range(1, n_row)]
        + [place.to_text(dy, dz) for dy in range(1, ring) for dz in range(ring)]
        + [
            {
                "row": place.z * ring + place.along_x(step),
                "col": place.y * 2 + 1 - place.core,
            }
            for step in range(ring)
        ]
        + [place.across(step) for step in range(ring)]
    )


class AlongX:
    def __init__(self, mail, place, ref, first=0, count=None):
        self.mail, self.place, self.ref = mail, place, ref
        self.first, self.count = first, count or ref.shape[1]
        self.half = self.count // 2

    def whole(self, index):
        return self.ref.at[index, pl.ds(self.first, self.count)]

    def block(self, step, core):
        return self.place.along_x(step) * 2 + core

    def lower(self, index):
        return self.ref.at[index, pl.ds(self.first, self.half)]

    def upper(self, index):
        return self.ref.at[index, pl.ds(self.first + self.half, self.half)]

    def start(self):
        place, mail = self.place, self.mail
        own = self.whole(place.slot)
        self.up = mail.push(own, own, place.to_x(1))
        self.down = mail.push(own, own, place.to_x(-1))
        self.over = [mail.push(own, own, place.sibling())]

    def forward(self):
        place, mail = self.place, self.mail
        below = self.block(-1, place.core)
        mail.got(self.whole(below), self.up)
        self.up_half = mail.push(self.lower(below), self.lower(below), place.to_x(1))
        self.over.append(mail.push(self.whole(below), self.whole(below), place.sibling()))
        above = self.block(1, place.core)
        mail.got(self.whole(above), self.down)
        self.down_half = mail.push(self.upper(above), self.upper(above), place.to_x(-1))
        self.over.append(mail.push(self.whole(above), self.whole(above), place.sibling()))

    def last(self):
        place, mail = self.place, self.mail
        far = self.block(2, place.core)
        mail.got(self.lower(far), self.up_half)
        self.over.append(mail.push(self.lower(far), self.lower(far), place.sibling()))
        mail.got(self.upper(far), self.down_half)
        self.over.append(mail.push(self.upper(far), self.upper(far), place.sibling()))

    def end(self):
        place, mail = self.place, self.mail
        other = 1 - place.core
        mail.got(self.whole(self.block(0, other)), self.over[0])
        mail.got(self.whole(self.block(-1, other)), self.over[1])
        mail.got(self.whole(self.block(1, other)), self.over[2])
        far = self.block(2, other)
        mail.got(self.lower(far), self.over[3])
        mail.got(self.upper(far), self.over[4])


def step_kernel(
    si_hbm,
    sp_hbm,
    st_hbm,
    ti_hbm,
    pt_hbm,
    tt_hbm,
    order_hbm,
    pair_hbm,
    embed_out,
    proj_out,
    si_ref,
    sp_ref,
    st_ref,
    ti_ref,
    tt_ref,
    text,
    img_s,
    img_t,
    pairs,
    raw_ref,
    orders,
    feat_out,
    feat_in,
    proj,
    embed,
    scores,
    row_high,
    row_total,
    col_high,
    col_total,
    row_stats,
    row_landed,
    row_lse,
    col_stats,
    col_landed,
    col_lse,
    row_tiles,
    offsets,
    partial_grad,
    from_core,
    leaving,
    arriving,
    si_sibling,
    grads,
    grads_sibling,
    summed,
    first_out,
    first_in,
    second,
    second_out,
    second_in,
    third,
    third_in,
    group_sums,
    gathered,
    load_sem,
    send_sem,
    recv_sem,
):
    place = Place()
    mail = Mail(send_sem, recv_sem)
    row, col, core, slot = place.row, place.col, place.core, place.slot
    other = 1 - core
    per_device, width = st_ref.shape
    teacher_width = tt_ref.shape[1]
    half = per_device // 2
    share = si_ref.shape[1] // 2

    loads = []
    for source, target in (
        (order_hbm, orders.at[row]),
        (pt_hbm, proj.at[slot, place.y * ring + place.z]),
        (pair_hbm, pairs.at[slot]),
        (st_hbm, st_ref),
        (tt_hbm, tt_ref),
        (si_hbm, si_ref),
        (sp_hbm, sp_ref),
        (ti_hbm, ti_ref),
    ):
        copy = pltpu.make_async_copy(source, target, load_sem.at[len(loads)])
        copy.start()
        loads.append(copy)
    barrier = pltpu.get_barrier_semaphore()
    peers = all_peers(place)
    for device in peers:
        pl.semaphore_signal(barrier, inc=1, device_id=device, device_id_type=MESH)
    for copy in loads[:5]:
        copy.wait()
    own_y, own_z = place.y, place.z
    text[own_z, own_y, :, :teacher_width] = unit_rows(tt_ref[...].astype(jnp.float32)).astype(
        jnp.bfloat16
    )
    text[own_z, own_y, :, teacher_width:] = unit_rows(st_ref[...].astype(jnp.float32)).astype(
        jnp.bfloat16
    )
    pl.semaphore_wait(barrier, len(peers))

    own_proj = proj.at[slot, place.y * ring + place.z]
    proj_z = [mail.push(own_proj, own_proj, place.to_z(step)) for step in (1, 3, 2)]

    def block(dy, dz, part):
        return text.at[place.along_z(dz), place.along_y(dy), pl.ds(part * half, half)]

    z_up, z_down, y_up, y_down, y_on = {}, {}, {}, {}, {}

    def start_z(part):
        z_up[part] = mail.push(block(0, 0, part), block(0, 0, part), place.to_z(1))
        z_down[part] = mail.push(block(0, 0, part), block(0, 0, part), place.to_z(-1))

    def start_y(dz, part):
        y_up[dz, part] = mail.push(block(0, dz, part), block(0, dz, part), place.to_y(1))
        y_down[dz, part] = mail.push(block(0, dz, part), block(0, dz, part), place.to_y(-1))

    def forward_y(dz):
        mail.got(block(-1, dz, 0), y_up[dz, 0])
        y_on[dz, 0] = mail.push(block(-1, dz, 0), block(-1, dz, 0), place.to_y(1))
        mail.got(block(1, dz, 1), y_down[dz, 1])
        y_on[dz, 1] = mail.push(block(1, dz, 1), block(1, dz, 1), place.to_y(-1))

    start_z(0)
    start_y(0, 0)
    own_order = orders.at[row]
    order_mail = [
        mail.push(own_order, own_order, {"row": (row + step) % n_row}) for step in range(1, n_row)
    ]
    loads[5].wait()
    loads[6].wait()
    si_mail = mail.push(
        si_ref.at[:, pl.ds(pl.multiple_of(other * share, share), share)],
        si_sibling,
        place.sibling(),
    )
    raw_student = jnp.dot(si_ref[...], sp_ref[...], preferred_element_type=jnp.float32)
    raw_ref[...] = raw_student
    img_s[slot] = unit_rows(raw_student).astype(jnp.bfloat16)
    for step, ticket in zip((1, 3, 2), proj_z):
        mail.got(proj.at[slot, place.y * ring + place.along_z(-step)], ticket)

    def proj_rows(step, start=0, count=ring):
        return proj.at[slot, pl.ds(place.along_y(step) * ring + start, count)]

    def proj_spread(step):
        spread = AlongX(mail, place, proj, place.along_y(step) * ring, ring)
        spread.start()
        return spread

    proj_up = mail.push(proj_rows(0), proj_rows(0), place.to_y(1))
    proj_down = mail.push(proj_rows(0), proj_rows(0), place.to_y(-1))
    spreads = [proj_spread(0)]
    start_z(1)
    start_y(0, 1)
    student = AlongX(mail, place, img_s)
    student.start()
    own_pairs = pairs.at[slot]
    pair_mail = [mail.push(own_pairs, own_pairs, place.to_slot(step)) for step in range(1, n_col)]

    image_rows = 2 * per_device
    chunk = ring * per_device
    col_mail = {}

    def end_y(dz):
        mail.got(block(-1, dz, 1), y_up[dz, 1])
        mail.got(block(1, dz, 0), y_down[dz, 0])
        mail.got(block(2, dz, 0), y_on[dz, 0])
        mail.got(block(2, dz, 1), y_on[dz, 1])

    def prepare():
        end_y(0)
        for step in range(1, n_col):
            mail.got(pairs.at[(slot + n_col - step) % n_col], pair_mail[step - 1])
        lane_ids = lax.broadcasted_iota(jnp.int32, (per_device, per_device), 1)
        for source in range(n_col):
            wide = jnp.broadcast_to(pairs[source].astype(jnp.float32), (per_device, per_device)).T
            offsets[source * per_device : (source + 1) * per_device] = (
                wide.astype(jnp.int32) - lane_ids
            )
        row_high[...] = jnp.full(row_high.shape, lowest, jnp.float32)
        row_total[...] = jnp.zeros(row_total.shape, jnp.float32)
        col_stats[...] = jnp.zeros(col_stats.shape, jnp.float32)

    def text_student(index):
        return text[index, :, :, teacher_width:].reshape(chunk, width)

    def text_teacher(index):
        return text[index, :, :, :teacher_width].reshape(chunk, teacher_width)

    def process(kind, dz):
        index = place.along_z(dz)
        col_high[...] = jnp.full(col_high.shape, lowest, jnp.float32)
        col_total[...] = jnp.zeros(col_total.shape, jnp.float32)

        def images(step, carry):
            rows = pl.ds(pl.multiple_of(step * image_rows, image_rows), image_rows)
            if kind == 0:
                left = img_s[pl.ds(2 * step, 2)].reshape(image_rows, width)
                right = text_student(index)
            else:
                left = img_t[pl.ds(2 * step, 2)].reshape(image_rows, teacher_width)
                right = text_teacher(index)
            values = score_scale * lax.dot_general(
                left, right, nt_dims, preferred_element_type=jnp.float32
            )
            scores[kind, index, rows] = values
            tiles = [values[:, start : start + per_device] for start in range(0, chunk, per_device)]
            before = row_high[kind, rows]
            high = before
            for tile in tiles:
                high = jnp.maximum(high, tile)
            total = row_total[kind, rows] * jnp.exp2(before - high)
            for tile in tiles:
                total = total + jnp.exp2(tile - high)
            row_high[kind, rows] = high
            row_total[kind, rows] = total
            stacked = values.reshape(image_rows // 8, 8, chunk)
            before = col_high[...]
            high = jnp.maximum(before, jnp.max(stacked, axis=0))
            total = col_total[...] * jnp.exp2(before - high)
            col_total[...] = total + jnp.sum(jnp.exp2(stacked - high[None]), axis=0)
            col_high[...] = high
            return carry

        lax.fori_loop(0, ring, images, 0)
        high = jnp.max(col_high[...], axis=0, keepdims=True)
        total = jnp.sum(col_total[...] * jnp.exp2(col_high[...] - high), axis=0, keepdims=True)
        for y in range(ring):
            lane = slice(y * per_device, (y + 1) * per_device)
            col_stats[index, y, 2 * kind : 2 * kind + 1] = high[:, lane]
            col_stats[index, y, 2 * kind + 1 : 2 * kind + 2] = total[:, lane]
        if kind == 1:
            for dy in range(ring):
                y = place.along_y(dy)
                if dy or dz:
                    col_mail[dy, dz % ring] = mail.push(
                        col_stats.at[index, y],
                        col_landed.at[own_y, own_z],
                        place.to_text(dy, dz),
                    )
                else:
                    col_landed[own_y, own_z] = col_stats[index, y]

    loads[7].wait()
    for step in range(1, n_row):
        mail.got(orders.at[(row + n_row - step) % n_row], order_mail[step - 1])
    lanes = lax.broadcasted_iota(jnp.int32, (per_device, 2 * per_device), 1).astype(jnp.float32)

    def pick(target, carry):
        wanted = (orders[target] - col * (n_row * per_device)).astype(jnp.float32)
        wanted = jnp.broadcast_to(wanted, (per_device, per_device)).T
        wanted = jnp.concatenate([wanted, wanted], axis=1)
        total = jnp.zeros((per_device, ti_ref.shape[0]), jnp.float32)
        for start in range(0, n_row * per_device, 2 * per_device):
            chosen = jnp.where(wanted == lanes + float(start), 1.0, 0.0).astype(jnp.bfloat16)
            total += lax.dot_general(
                chosen,
                ti_ref[:, start : start + 2 * per_device],
                nt_dims,
                preferred_element_type=jnp.float32,
            )
        feat_out[target] = total.astype(jnp.bfloat16)
        return carry

    half_rows = ring // 2
    lower, upper = (0, half_rows), (half_rows, half_rows)
    lax.fori_loop(0, n_row // 2, pick, 0)
    mail.got(proj_rows(-1), proj_up)
    proj_up = mail.push(proj_rows(-1, *lower), proj_rows(-1, *lower), place.to_y(1))
    spreads.append(proj_spread(-1))
    mail.got(proj_rows(1), proj_down)
    proj_down = mail.push(proj_rows(1, *upper), proj_rows(1, *upper), place.to_y(-1))
    spreads.append(proj_spread(1))
    spreads[0].forward()
    lax.fori_loop(n_row // 2, n_row, pick, 0)
    feat_mail = []
    for step in range(1, n_row):
        target = (row + step) % n_row
        feat_mail.append(mail.push(feat_out.at[target], feat_in.at[row], {"row": target}))
    feat_in[row] = feat_out[row]
    mail.got(proj_rows(2, *lower), proj_up)
    mail.got(proj_rows(2, *upper), proj_down)
    spreads.append(proj_spread(2))

    mail.got(block(0, -1, 0), z_up[0])
    z_up_on = mail.push(block(0, -1, 0), block(0, -1, 0), place.to_z(1))
    start_y(-1, 0)
    mail.got(block(0, 1, 0), z_down[0])
    start_y(1, 0)
    forward_y(0)
    spreads[0].last()
    spreads[1].forward()
    spreads[2].forward()
    mail.got(block(0, 1, 1), z_down[1])
    z_down_on = mail.push(block(0, 1, 1), block(0, 1, 1), place.to_z(-1))
    start_y(1, 1)
    mail.got(block(0, -1, 1), z_up[1])
    start_y(-1, 1)
    spreads[1].last()
    spreads[2].last()
    spreads[3].forward()
    student.forward()
    spreads[3].last()
    student.last()
    student.end()
    prepare()
    process(0, 0)
    mail.got(block(0, 2, 0), z_up_on)
    start_y(2, 0)
    mail.got(block(0, 2, 1), z_down_on)
    start_y(2, 1)
    for spread in spreads:
        spread.end()
    for step in range(1, n_row):
        mail.got(feat_in.at[(row + n_row - step) % n_row], feat_mail[step - 1])
    proj_width = proj.shape[2]

    def project(source, carry):
        total = jnp.zeros((proj_width, per_device), jnp.float32)
        for features in range(n_row):
            z, x = features // ring, features % ring
            total += lax.dot_general(
                proj[x * 2 + source % 2, source // 2 * ring + z],
                feat_in[features],
                nt_dims,
                preferred_element_type=jnp.float32,
            )
        embed[pl.ds(pl.multiple_of(source * proj_width, 8), proj_width), :] = total
        return carry

    lax.fori_loop(0, n_col, project, 0)
    raw_teacher = embed[...]
    scale = lax.rsqrt(jnp.sum(raw_teacher * raw_teacher, axis=0, keepdims=True) + norm_eps)
    img_t[slot] = (raw_teacher * scale).T.astype(jnp.bfloat16)
    teacher = AlongX(mail, place, img_t)
    teacher.start()
    forward_y(-1)
    teacher.forward()
    forward_y(1)
    end_y(-1)
    process(0, -1)
    teacher.last()
    end_y(1)
    process(0, 1)
    forward_y(2)
    teacher.end()
    process(1, 0)
    process(1, -1)
    process(1, 1)
    end_y(2)
    process(0, 2)
    process(1, 2)

    for source in range(n_col):
        rows = slice(source * per_device, (source + 1) * per_device)
        found = []
        for kind in range(2):
            high_all = row_high[kind, rows].T
            high = jnp.max(high_all, axis=0, keepdims=True)
            total = jnp.sum(
                row_total[kind, rows].T * jnp.exp2(high_all - high), axis=0, keepdims=True
            )
            found += [high, total]
        row_stats[source] = jnp.concatenate(
            found + [jnp.zeros((4, per_device), jnp.float32)], axis=0
        )
    row_mail = [
        mail.push(
            row_stats.at[(slot + step) % n_col], row_landed.at[slot], place.to_slot(step)
        )
        for step in range(1, n_col)
    ]
    row_landed[slot] = row_stats[slot]

    def merge(parts):
        found = []
        for kind in range(2):
            high = jnp.max(parts[:, 2 * kind], axis=0, keepdims=True)
            total = jnp.sum(
                parts[:, 2 * kind + 1] * jnp.exp2(parts[:, 2 * kind] - high),
                axis=0,
                keepdims=True,
            )
            found.append(high + jnp.log2(total) + float(kind))
        return jnp.concatenate(found + [jnp.zeros((6, per_device), jnp.float32)], axis=0)

    pairs_of_steps = [(dy, dz) for dy in range(ring) for dz in range(ring) if dy or dz]
    for dy, dz in pairs_of_steps:
        mail.got(col_landed.at[place.along_y(-dy), place.along_z(-dz)], col_mail[dy, dz])
    col_lse[own_y, own_z] = merge(col_landed[...].reshape(n_row, 8, per_device))
    own_lse = col_lse.at[own_y, own_z]
    col_back = {
        (dy, dz): mail.push(own_lse, own_lse, place.to_text(dy, dz)) for dy, dz in pairs_of_steps
    }
    for step in range(1, n_col):
        mail.got(row_landed.at[(slot + n_col - step) % n_col], row_mail[step - 1])
    row_lse[slot] = merge(row_landed[...])
    row_back = [
        mail.push(row_lse.at[slot], row_lse.at[slot], place.to_slot(step))
        for step in range(1, n_col)
    ]
    for step in range(1, n_col):
        mail.got(row_lse.at[(slot + n_col - step) % n_col], row_back[step - 1])
    for source in range(n_col):
        rows = slice(source * per_device, (source + 1) * per_device)
        for kind in range(2):
            wide = row_lse[source, kind : kind + 1, :]
            row_tiles[kind, rows] = jnp.broadcast_to(wide, (per_device, per_device)).T
    for dy, dz in pairs_of_steps:
        mail.got(col_lse.at[place.along_y(-dy), place.along_z(-dz)], col_back[dy, dz])

    over = {}
    across = {}

    def weigh(step):
        target = place.along_x(step)
        rows = pl.ds(pl.multiple_of(target * image_rows, image_rows), image_rows)
        partial_grad[target] = jnp.zeros(partial_grad.shape[1:], jnp.float32)

        def texts(index, carry):
            parts = []
            for y in range(ring):
                lane = slice(y * per_device, (y + 1) * per_device)
                student_scores = scores[0, index, rows, lane]
                teacher_scores = scores[1, index, rows, lane]
                first_id = ((index * ring + place.x) * n_col + y * 2 + core) * per_device
                matched = jnp.where(offsets[rows] == first_id, 1.0, 0.0)
                weights = (
                    jnp.exp2(student_scores - row_tiles[0, rows])
                    + jnp.exp2(student_scores - col_lse[y, index, 0:1, :])
                    - jnp.exp2(teacher_scores - row_tiles[1, rows])
                    - jnp.exp2(teacher_scores - col_lse[y, index, 1:2, :])
                    - matched
                )
                parts.append(weights.astype(jnp.bfloat16))
            product = jnp.dot(
                jnp.concatenate(parts, axis=1),
                text_student(index),
                preferred_element_type=jnp.float32,
            )
            partial_grad[target] += product.reshape(2, per_device, width)
            return carry

        lax.fori_loop(0, ring, texts, 0)
        over[step] = mail.push(
            partial_grad.at[target, other], from_core.at[target], place.sibling()
        )

    def pass_over(step):
        target = place.along_x(step)
        mail.got(from_core.at[target], over[step])
        total = partial_grad[target, core] + from_core[target]
        if step:
            leaving[step - 1] = total.astype(jnp.bfloat16)
            across[step] = mail.push(
                leaving.at[step - 1], arriving.at[step - 1], place.to_x(step)
            )
        return total

    weigh(2)
    weigh(1)
    pass_over(2)
    weigh(3)
    pass_over(1)
    weigh(0)
    pass_over(3)
    embed_grad = pass_over(0)
    for step in (2, 1, 3):
        mail.got(arriving.at[step - 1], across[step])
        embed_grad = embed_grad + arriving[step - 1].astype(jnp.float32)
    embed_grad = logit_scale * embed_grad
    raw_student = raw_ref[...]
    scale = lax.rsqrt(jnp.sum(raw_student * raw_student, axis=1, keepdims=True) + norm_eps)
    student_unit = raw_student * scale
    inner_term = jnp.sum(student_unit * embed_grad, axis=1, keepdims=True)
    grad_embed = (embed_grad - student_unit * inner_term) * scale
    embed_out[...] = grad_embed
    grads[...] = grad_embed.astype(jnp.bfloat16)
    ticket = mail.push(grads, grads_sibling, place.sibling())

    pieces, kinds, size = summed.shape[:3]
    for kind in range(kinds):
        start = pl.multiple_of(core * share + kind * size, size)
        product = lax.dot_general(
            si_ref[:, pl.ds(start, size)],
            grads[...],
            tn_dims,
            preferred_element_type=jnp.float32,
        )
        for lane in range(pieces):
            summed[lane, kind] = product[:, lane * size : (lane + 1) * size]
    mail.got(si_sibling, si_mail)
    mail.got(grads_sibling, ticket)
    for kind in range(kinds):
        product = lax.dot_general(
            si_sibling[:, kind * size : (kind + 1) * size],
            grads_sibling[...],
            tn_dims,
            preferred_element_type=jnp.float32,
        )
        for lane in range(pieces):
            total = summed[lane, kind] + product[:, lane * size : (lane + 1) * size]
            summed[lane, kind] = total
            first_out[lane, kind] = total.astype(jnp.bfloat16)

    along_x = (place.x, place.along_x, place.to_x)
    along_y = (place.y, place.along_y, place.to_y)
    families = ((pl.ds(0, 2), along_y, along_x), (pl.ds(2, 1), along_x, along_y))
    quarter, tile = size // ring, size // n_row
    steps = (2, 1, 3)

    def rows_of(position, count):
        return pl.ds(pl.multiple_of(position * count, count), count)

    tickets = {}
    for index, (chosen, (own, at, to), _) in enumerate(families):
        for step in steps:
            tickets[index, step] = mail.push(
                first_out.at[at(step), chosen], first_in.at[step - 1, chosen], to(step)
            )
    for index, (chosen, (own, at, to), (own_next, at_next, to_next)) in enumerate(families):
        total = summed[own, chosen]
        for step in steps:
            mail.got(first_in.at[step - 1, chosen], tickets[index, step])
            total = total + first_in[step - 1, chosen].astype(jnp.float32)
        second[chosen] = total
        second_out[chosen] = total.astype(jnp.bfloat16)
        for step in steps:
            tickets[index, step] = mail.push(
                second_out.at[chosen, rows_of(at_next(step), quarter)],
                second_in.at[step - 1, chosen],
                to_next(step),
            )
    for index, (chosen, _, (own, at, to)) in enumerate(families):
        total = second[chosen, rows_of(own, quarter)]
        for step in steps:
            mail.got(second_in.at[step - 1, chosen], tickets[index, step])
            total = total + second_in[step - 1, chosen].astype(jnp.float32)
        third[chosen] = total
    for step in steps:
        tickets[step] = mail.push(
            third.at[:, rows_of(place.along_z(step), tile)], third_in.at[step - 1], place.to_z(step)
        )
    total = third[:, rows_of(place.z, tile)]
    for step in steps:
        mail.got(third_in.at[step - 1], tickets[step])
        total = total + third_in[step - 1]
    group = lax.axis_index("group")

    def group_tile(side, step):
        return group_sums.at[side, :, rows_of(place.along_z(step), tile)]

    group_tile(group, 0)[...] = total
    own_tile = group_tile(group, 0)
    for step in steps:
        tickets[0, step] = mail.push(own_tile, own_tile, place.to_z(step))
    for step in range(ring):
        tickets[1, step] = mail.push(own_tile, own_tile, place.across(step))
    for step in steps:
        mail.got(group_tile(group, -step), tickets[0, step])
    for step in range(ring):
        mail.got(group_tile(1 - group, -step), tickets[1, step])
    total = (group_sums[0] + group_sums[1]).astype(jnp.bfloat16)

    for index, (chosen, (own1, at1, to1), (own2, at2, to2)) in enumerate(families):
        mine = gathered.at[core, own1, chosen, rows_of(own2, quarter)]
        mine[...] = total[chosen.start : chosen.start + chosen.size]
        for step in steps:
            tickets[index, step] = mail.push(mine, mine, to2(step))
    back = {}
    for index, (chosen, (own1, at1, to1), (own2, at2, to2)) in enumerate(families):
        for step in steps:
            mail.got(
                gathered.at[core, own1, chosen, rows_of(at2(-step), quarter)],
                tickets[index, step],
            )
        mine = gathered.at[core, own1, chosen]
        for step in steps:
            tickets[index, step] = mail.push(mine, mine, to1(step))
        back[index, 0] = mail.push(mine, mine, place.sibling())
    for step in (1, 3, 2):
        for index, (chosen, (own1, at1, to1), _) in enumerate(families):
            theirs = gathered.at[core, at1(-step), chosen]
            mail.got(theirs, tickets[index, step])
            back[index, step] = mail.push(theirs, theirs, place.sibling())

    def write(side):
        for kind in range(kinds):
            rows = pl.ds(pl.multiple_of((side * kinds + kind) * size, size), size)
            for lane in range(pieces):
                proj_out[rows, lane * size : (lane + 1) * size] = gathered[
                    side, lane, kind
                ].astype(jnp.float32)

    write(core)
    for step in (0, 1, 3, 2):
        for index, (chosen, (own1, at1, to1), _) in enumerate(families):
            mail.got(gathered.at[other, at1(-step), chosen], back[index, step])
    write(other)
    mail.finish()


def body(
    student_image,
    student_proj,
    student_text,
    teacher_image,
    teacher_proj,
    teacher_text,
    assignment,
    pair_ids,
):
    per_device, width = student_text.shape
    teacher_width = teacher_text.shape[1]
    student_width = student_image.shape[1]
    features, proj_width = teacher_proj.shape
    size = 128
    kinds = student_width // (2 * size)
    pieces = width // size
    bf16, f32, i32 = jnp.bfloat16, jnp.float32, jnp.int32
    tile = (8, per_device)
    chunk = ring * per_device
    images = n_col * per_device
    hbm = pl.BlockSpec(memory_space=pl.ANY)
    vmem = pl.BlockSpec(memory_space=pltpu.VMEM)
    copies = 230
    grad_embed, grad_proj = pl.pallas_call(
        step_kernel,
        out_shape=(
            jax.ShapeDtypeStruct((per_device, width), f32),
            jax.ShapeDtypeStruct((student_width, width), f32),
        ),
        in_specs=[hbm] * 8,
        out_specs=[vmem] * 2,
        scratch_shapes=[
            pltpu.VMEM(student_image.shape, bf16),
            pltpu.VMEM(student_proj.shape, bf16),
            pltpu.VMEM(student_text.shape, bf16),
            pltpu.VMEM((features, n_row * per_device), bf16),
            pltpu.VMEM(teacher_text.shape, bf16),
            pltpu.VMEM((ring, ring, per_device, teacher_width + width), bf16),
            pltpu.VMEM((n_col, per_device, width), bf16),
            pltpu.VMEM((n_col, per_device, teacher_width), bf16),
            pltpu.VMEM((n_col, 1, per_device), i32),
            pltpu.VMEM((per_device, width), f32),
            pltpu.VMEM((n_row, 1, per_device), i32),
            pltpu.VMEM((n_row, per_device, features), bf16),
            pltpu.VMEM((n_row, per_device, features), bf16),
            pltpu.VMEM((n_col, n_row, proj_width, features), bf16),
            pltpu.VMEM((teacher_width, per_device), f32),
            pltpu.VMEM((2, ring, images, chunk), f32),
            pltpu.VMEM((2, images, per_device), f32),
            pltpu.VMEM((2, images, per_device), f32),
            pltpu.VMEM((8, chunk), f32),
            pltpu.VMEM((8, chunk), f32),
            pltpu.VMEM((n_col,) + tile, f32),
            pltpu.VMEM((n_col,) + tile, f32),
            pltpu.VMEM((n_col,) + tile, f32),
            pltpu.VMEM((ring, ring) + tile, f32),
            pltpu.VMEM((ring, ring) + tile, f32),
            pltpu.VMEM((ring, ring) + tile, f32),
            pltpu.VMEM((2, images, per_device), f32),
            pltpu.VMEM((images, per_device), i32),
            pltpu.VMEM((ring, 2, per_device, width), f32),
            pltpu.VMEM((ring, per_device, width), f32),
            pltpu.VMEM((ring - 1, per_device, width), bf16),
            pltpu.VMEM((ring - 1, per_device, width), bf16),
            pltpu.VMEM((per_device, student_width // 2), bf16),
            pltpu.VMEM((per_device, width), bf16),
            pltpu.VMEM((per_device, width), bf16),
            pltpu.VMEM((pieces, kinds, size, size), f32),
            pltpu.VMEM((pieces, kinds, size, size), bf16),
            pltpu.VMEM((ring - 1, kinds, size, size), bf16),
            pltpu.VMEM((kinds, size, size), f32),
            pltpu.VMEM((kinds, size, size), bf16),
            pltpu.VMEM((ring - 1, kinds, size // 4, size), bf16),
            pltpu.VMEM((kinds, size // 4, size), f32),
            pltpu.VMEM((ring - 1, kinds, 8, size), f32),
            pltpu.VMEM((2, kinds, size // 4, size), f32),
            pltpu.VMEM((2, pieces, kinds, size, size), bf16),
            pltpu.SemaphoreType.DMA((8,)),
            pltpu.SemaphoreType.DMA((96,)),
            pltpu.SemaphoreType.DMA((copies,)),
        ],
        compiler_params=pltpu.CompilerParams(
            collective_id=0, has_side_effects=True, vmem_limit_bytes=60 * 1024 * 1024
        ),
    )(
        student_image,
        student_proj,
        student_text,
        teacher_image.T,
        teacher_proj.T,
        teacher_text,
        assignment,
        pair_ids,
    )
    return grad_embed, grad_proj


def solution(mesh):
    placed = (
        P(("group", "row", "col"), None),
        P(),
        P(("group", "row", "col"), None),
        P(("group", "col"), "row"),
        P("row", "col"),
        P(("group", "row", "col"), None),
        P("group", ("row", "col")),
        P("group", ("row", "col")),
    )
    return jax.shard_map(
        body,
        mesh=mesh,
        in_specs=placed,
        out_specs=(P(("group", "row", "col"), None), P()),
        check_vma=False,
    )
```

```python
import math

import jax
import jax.numpy as jnp
from jax import lax
from jax.experimental import pallas as pl
from jax.experimental.pallas import tpu as pltpu
from jax.sharding import PartitionSpec as P

logit_scale = 100.0
score_scale = logit_scale * math.log2(math.e)
lowest = -1e30
norm_eps = 1e-06
MESH = pl.DeviceIdType.MESH
ring = 4
n_row = 16
n_col = 8
nt_dims = (((1,), (1,)), ((), ()))
tn_dims = (((0,), (0,)), ((), ()))


def unit_rows(values):
    return values * lax.rsqrt(jnp.sum(values * values, axis=1, keepdims=True) + norm_eps)


class Place:
    def __init__(self):
        self.row = lax.axis_index("row")
        self.col = lax.axis_index("col")
        self.z, self.x = self.row // ring, self.row % ring
        self.y, self.core = self.col // 2, self.col % 2
        self.slot = self.x * 2 + self.core

    def along_x(self, step):
        return (self.x + step + ring) % ring

    def along_y(self, step):
        return (self.y + step + ring) % ring

    def along_z(self, step):
        return (self.z + step + ring) % ring

    def to_x(self, step):
        return {"row": self.z * ring + self.along_x(step)}

    def to_z(self, step):
        return {"row": self.along_z(step) * ring + self.x}

    def to_y(self, step):
        return {"col": self.along_y(step) * 2 + self.core}

    def to_slot(self, step):
        slot = (self.slot + step) % n_col
        return {"row": self.z * ring + slot // 2, "col": self.y * 2 + slot % 2}

    def to_text(self, dy, dz):
        return {
            "row": self.along_z(dz) * ring + self.x,
            "col": self.along_y(dy) * 2 + self.core,
        }

    def across(self, step):
        return {
            "group": 1 - lax.axis_index("group"),
            "row": self.along_z(step) * ring + self.x,
        }

    def sibling(self):
        return {"col": self.y * 2 + 1 - self.core}


class Mail:
    def __init__(self, send_sem, recv_sem):
        self.send_sem, self.recv_sem = send_sem, recv_sem
        self.used = 0
        self.sent = {}

    def push(self, src, dst, device):
        index = self.used
        self.used += 1
        turn = index % self.send_sem.shape[0]
        if turn in self.sent:
            self.sent[turn].wait_send()
        copy = pltpu.make_async_remote_copy(
            src_ref=src,
            dst_ref=dst,
            send_sem=self.send_sem.at[turn],
            recv_sem=self.recv_sem.at[index],
            device_id=device,
            device_id_type=MESH,
        )
        copy.start()
        self.sent[turn] = copy
        return index, device

    def got(self, slot, ticket):
        index, device = ticket
        pltpu.make_async_remote_copy(
            src_ref=slot,
            dst_ref=slot,
            send_sem=self.send_sem.at[0],
            recv_sem=self.recv_sem.at[index],
            device_id=device,
            device_id_type=MESH,
        ).wait_recv()

    def finish(self):
        for copy in self.sent.values():
            copy.wait_send()


def all_peers(place):
    return (
        [{"row": (place.row + step) % n_row} for step in range(1, n_row)]
        + [place.to_text(dy, dz) for dy in range(1, ring) for dz in range(ring)]
        + [
            {
                "row": place.z * ring + place.along_x(step),
                "col": place.y * 2 + 1 - place.core,
            }
            for step in range(ring)
        ]
        + [place.across(step) for step in range(ring)]
    )


class AlongX:
    def __init__(self, mail, place, ref, first=0, count=None):
        self.mail, self.place, self.ref = mail, place, ref
        self.first, self.count = first, count or ref.shape[1]
        self.half = self.count // 2

    def whole(self, index):
        return self.ref.at[index, pl.ds(self.first, self.count)]

    def block(self, step, core):
        return self.place.along_x(step) * 2 + core

    def lower(self, index):
        return self.ref.at[index, pl.ds(self.first, self.half)]

    def upper(self, index):
        return self.ref.at[index, pl.ds(self.first + self.half, self.half)]

    def start(self):
        place, mail = self.place, self.mail
        own = self.whole(place.slot)
        self.up = mail.push(own, own, place.to_x(1))
        self.down = mail.push(own, own, place.to_x(-1))
        self.over = [mail.push(own, own, place.sibling())]

    def forward(self):
        place, mail = self.place, self.mail
        below = self.block(-1, place.core)
        mail.got(self.whole(below), self.up)
        self.up_half = mail.push(self.lower(below), self.lower(below), place.to_x(1))
        self.over.append(mail.push(self.whole(below), self.whole(below), place.sibling()))
        above = self.block(1, place.core)
        mail.got(self.whole(above), self.down)
        self.down_half = mail.push(self.upper(above), self.upper(above), place.to_x(-1))
        self.over.append(mail.push(self.whole(above), self.whole(above), place.sibling()))

    def last(self):
        place, mail = self.place, self.mail
        far = self.block(2, place.core)
        mail.got(self.lower(far), self.up_half)
        self.over.append(mail.push(self.lower(far), self.lower(far), place.sibling()))
        mail.got(self.upper(far), self.down_half)
        self.over.append(mail.push(self.upper(far), self.upper(far), place.sibling()))

    def end(self):
        place, mail = self.place, self.mail
        other = 1 - place.core
        mail.got(self.whole(self.block(0, other)), self.over[0])
        mail.got(self.whole(self.block(-1, other)), self.over[1])
        mail.got(self.whole(self.block(1, other)), self.over[2])
        far = self.block(2, other)
        mail.got(self.lower(far), self.over[3])
        mail.got(self.upper(far), self.over[4])


def step_kernel(
    si_hbm,
    sp_hbm,
    st_hbm,
    ti_hbm,
    pt_hbm,
    tt_hbm,
    order_hbm,
    pair_hbm,
    embed_out,
    gathered,
    si_ref,
    sp_ref,
    st_ref,
    ti_ref,
    tt_ref,
    text,
    img_s,
    img_t,
    pairs,
    raw_ref,
    orders,
    feat_out,
    feat_in,
    proj,
    embed,
    scores,
    row_high,
    row_total,
    col_high,
    col_total,
    row_stats,
    row_landed,
    row_lse,
    col_stats,
    col_landed,
    col_lse,
    row_tiles,
    offsets,
    partial_grad,
    from_core,
    leaving,
    arriving,
    si_sibling,
    grads,
    grads_sibling,
    summed,
    first_out,
    first_in,
    second,
    second_out,
    second_in,
    third,
    third_in,
    group_sums,
    load_sem,
    send_sem,
    recv_sem,
):
    place = Place()
    mail = Mail(send_sem, recv_sem)
    row, col, core, slot = place.row, place.col, place.core, place.slot
    other = 1 - core
    per_device, width = st_ref.shape
    teacher_width = tt_ref.shape[1]
    first_part, second_part = 3 * per_device // 8, per_device // 2
    share = si_ref.shape[1] // 2

    barrier = pltpu.get_barrier_semaphore()
    peers = all_peers(place)
    for device in peers:
        pl.semaphore_signal(barrier, inc=1, device_id=device, device_id_type=MESH)
    loads = []
    for source, target in (
        (order_hbm, orders.at[row]),
        (pt_hbm, proj.at[slot, place.y * ring + place.z]),
        (pair_hbm, pairs.at[slot]),
        (st_hbm, st_ref),
        (tt_hbm, tt_ref),
        (si_hbm, si_ref),
        (sp_hbm, sp_ref),
        (ti_hbm, ti_ref),
    ):
        copy = pltpu.make_async_copy(source, target, load_sem.at[len(loads)])
        copy.start()
        loads.append(copy)
    for copy in loads[:5]:
        copy.wait()
    own_y, own_z = place.y, place.z
    text[own_z, own_y, :, :teacher_width] = unit_rows(tt_ref[...].astype(jnp.float32)).astype(
        jnp.bfloat16
    )
    text[own_z, own_y, :, teacher_width:] = unit_rows(st_ref[...].astype(jnp.float32)).astype(
        jnp.bfloat16
    )
    pl.semaphore_wait(barrier, len(peers))

    own_proj = proj.at[slot, place.y * ring + place.z]
    proj_z = [mail.push(own_proj, own_proj, place.to_z(step)) for step in (1, 3, 2)]

    def block(dy, dz, part):
        start, count = ((0, first_part), (first_part, second_part))[part]
        return text.at[place.along_z(dz), place.along_y(dy), pl.ds(start, count)]

    def last_rows(dz, first_y, count):
        return text.at[
            place.along_z(dz),
            pl.ds(first_y, count),
            pl.ds(first_part + second_part, per_device - first_part - second_part),
        ]

    z_up, z_down, y_up, y_down, y_on = {}, {}, {}, {}, {}

    def start_z(part):
        z_up[part] = mail.push(block(0, 0, part), block(0, 0, part), place.to_z(1))
        z_down[part] = mail.push(block(0, 0, part), block(0, 0, part), place.to_z(-1))

    def start_y(dz, part):
        y_up[dz, part] = mail.push(block(0, dz, part), block(0, dz, part), place.to_y(1))
        y_down[dz, part] = mail.push(block(0, dz, part), block(0, dz, part), place.to_y(-1))

    def forward_y(dz):
        mail.got(block(-1, dz, 0), y_up[dz, 0])
        y_on[dz, 0] = mail.push(block(-1, dz, 0), block(-1, dz, 0), place.to_y(1))
        mail.got(block(1, dz, 1), y_down[dz, 1])
        y_on[dz, 1] = mail.push(block(1, dz, 1), block(1, dz, 1), place.to_y(-1))

    start_z(0)
    own_last = last_rows(0, own_y, 1)
    last_y = [mail.push(own_last, own_last, place.to_y(step)) for step in (1, 3, 2)]
    start_y(0, 0)
    own_order = orders.at[row]
    order_mail = [
        mail.push(own_order, own_order, {"row": (row + step) % n_row}) for step in range(1, n_row)
    ]
    loads[5].wait()
    loads[6].wait()
    si_mail = mail.push(
        si_ref.at[:, pl.ds(pl.multiple_of(other * share, share), share)],
        si_sibling,
        place.sibling(),
    )
    raw_student = jnp.dot(si_ref[...], sp_ref[...], preferred_element_type=jnp.float32)
    raw_ref[...] = raw_student
    img_s[slot] = unit_rows(raw_student).astype(jnp.bfloat16)
    for step, ticket in zip((1, 3, 2), proj_z):
        mail.got(proj.at[slot, place.y * ring + place.along_z(-step)], ticket)

    def proj_rows(step, start=0, count=ring):
        return proj.at[slot, pl.ds(place.along_y(step) * ring + start, count)]

    def proj_spread(step):
        spread = AlongX(mail, place, proj, place.along_y(step) * ring, ring)
        spread.start()
        return spread

    proj_up = mail.push(proj_rows(0), proj_rows(0), place.to_y(1))
    proj_down = mail.push(proj_rows(0), proj_rows(0), place.to_y(-1))
    spreads = [proj_spread(0)]
    start_z(1)
    start_y(0, 1)
    student = AlongX(mail, place, img_s)
    student.start()
    own_pairs = pairs.at[slot]
    pair_mail = [mail.push(own_pairs, own_pairs, place.to_slot(step)) for step in range(1, n_col)]

    image_rows = 2 * per_device
    chunk = ring * per_device
    col_mail = {}

    def end_y(dz):
        mail.got(block(-1, dz, 1), y_up[dz, 1])
        mail.got(block(1, dz, 0), y_down[dz, 0])
        mail.got(block(2, dz, 0), y_on[dz, 0])
        mail.got(block(2, dz, 1), y_on[dz, 1])

    def prepare():
        end_y(0)
        for step in range(1, n_col):
            mail.got(pairs.at[(slot + n_col - step) % n_col], pair_mail[step - 1])
        lane_ids = lax.broadcasted_iota(jnp.int32, (per_device, per_device), 1)
        for source in range(n_col):
            wide = jnp.broadcast_to(pairs[source].astype(jnp.float32), (per_device, per_device)).T
            offsets[source * per_device : (source + 1) * per_device] = (
                wide.astype(jnp.int32) - lane_ids
            )
        row_high[...] = jnp.full(row_high.shape, lowest, jnp.float32)
        row_total[...] = jnp.zeros(row_total.shape, jnp.float32)
        col_stats[...] = jnp.zeros(col_stats.shape, jnp.float32)

    def text_student(index):
        return text[index, :, :, teacher_width:].reshape(chunk, width)

    def text_teacher(index):
        return text[index, :, :, :teacher_width].reshape(chunk, teacher_width)

    def process(kind, dz):
        index = place.along_z(dz)
        col_high[...] = jnp.full(col_high.shape, lowest, jnp.float32)
        col_total[...] = jnp.zeros(col_total.shape, jnp.float32)

        def images(step, carry):
            rows = pl.ds(pl.multiple_of(step * image_rows, image_rows), image_rows)
            if kind == 0:
                left = img_s[pl.ds(2 * step, 2)].reshape(image_rows, width)
                right = text_student(index)
            else:
                left = img_t[pl.ds(2 * step, 2)].reshape(image_rows, teacher_width)
                right = text_teacher(index)
            values = score_scale * lax.dot_general(
                left, right, nt_dims, preferred_element_type=jnp.float32
            )
            scores[kind, index, rows] = values
            tiles = [values[:, start : start + per_device] for start in range(0, chunk, per_device)]
            before = row_high[kind, rows]
            high = before
            for tile in tiles:
                high = jnp.maximum(high, tile)
            total = row_total[kind, rows] * jnp.exp2(before - high)
            for tile in tiles:
                total = total + jnp.exp2(tile - high)
            row_high[kind, rows] = high
            row_total[kind, rows] = total
            stacked = values.reshape(image_rows // 8, 8, chunk)
            before = col_high[...]
            high = jnp.maximum(before, jnp.max(stacked, axis=0))
            total = col_total[...] * jnp.exp2(before - high)
            col_total[...] = total + jnp.sum(jnp.exp2(stacked - high[None]), axis=0)
            col_high[...] = high
            return carry

        lax.fori_loop(0, ring, images, 0)
        high = jnp.max(col_high[...], axis=0, keepdims=True)
        total = jnp.sum(col_total[...] * jnp.exp2(col_high[...] - high), axis=0, keepdims=True)
        for y in range(ring):
            lane = slice(y * per_device, (y + 1) * per_device)
            col_stats[index, y, 2 * kind : 2 * kind + 1] = high[:, lane]
            col_stats[index, y, 2 * kind + 1 : 2 * kind + 2] = total[:, lane]
        if kind == 1:
            for dy in range(ring):
                y = place.along_y(dy)
                if dy or dz:
                    col_mail[dy, dz % ring] = mail.push(
                        col_stats.at[index, y],
                        col_landed.at[own_y, own_z],
                        place.to_text(dy, dz),
                    )
                else:
                    col_landed[own_y, own_z] = col_stats[index, y]

    loads[7].wait()
    for step in range(1, n_row):
        mail.got(orders.at[(row + n_row - step) % n_row], order_mail[step - 1])
    lanes = lax.broadcasted_iota(jnp.int32, (per_device, 2 * per_device), 1).astype(jnp.float32)

    def pick(target, carry):
        wanted = (orders[target] - col * (n_row * per_device)).astype(jnp.float32)
        wanted = jnp.broadcast_to(wanted, (per_device, per_device)).T
        wanted = jnp.concatenate([wanted, wanted], axis=1)
        total = jnp.zeros((per_device, ti_ref.shape[0]), jnp.float32)
        for start in range(0, n_row * per_device, 2 * per_device):
            chosen = jnp.where(wanted == lanes + float(start), 1.0, 0.0).astype(jnp.bfloat16)
            total += lax.dot_general(
                chosen,
                ti_ref[:, start : start + 2 * per_device],
                nt_dims,
                preferred_element_type=jnp.float32,
            )
        feat_out[target] = total.astype(jnp.bfloat16)
        return carry

    half_rows = ring // 2
    lower, upper = (0, half_rows), (half_rows, half_rows)
    lax.fori_loop(0, n_row // 2, pick, 0)
    mail.got(proj_rows(-1), proj_up)
    proj_up = mail.push(proj_rows(-1, *lower), proj_rows(-1, *lower), place.to_y(1))
    spreads.append(proj_spread(-1))
    mail.got(proj_rows(1), proj_down)
    proj_down = mail.push(proj_rows(1, *upper), proj_rows(1, *upper), place.to_y(-1))
    spreads.append(proj_spread(1))
    spreads[0].forward()
    lax.fori_loop(n_row // 2, n_row, pick, 0)
    feat_mail = []
    for step in range(1, n_row):
        target = (row + step) % n_row
        feat_mail.append(mail.push(feat_out.at[target], feat_in.at[row], {"row": target}))
    feat_in[row] = feat_out[row]
    mail.got(proj_rows(2, *lower), proj_up)
    mail.got(proj_rows(2, *upper), proj_down)
    spreads.append(proj_spread(2))

    mail.got(block(0, -1, 0), z_up[0])
    z_up_on = mail.push(block(0, -1, 0), block(0, -1, 0), place.to_z(1))
    start_y(-1, 0)
    mail.got(block(0, 1, 0), z_down[0])
    start_y(1, 0)
    forward_y(0)
    spreads[0].last()
    spreads[1].forward()
    spreads[2].forward()
    mail.got(block(0, 1, 1), z_down[1])
    z_down_on = mail.push(block(0, 1, 1), block(0, 1, 1), place.to_z(-1))
    start_y(1, 1)
    mail.got(block(0, -1, 1), z_up[1])
    start_y(-1, 1)
    for step, ticket in zip((1, 3, 2), last_y):
        mail.got(last_rows(0, place.along_y(-step), 1), ticket)
    last_up = mail.push(last_rows(0, 0, ring), last_rows(0, 0, ring), place.to_z(1))
    last_down = mail.push(last_rows(0, 0, ring), last_rows(0, 0, ring), place.to_z(-1))
    spreads[1].last()
    spreads[2].last()
    spreads[3].forward()
    student.forward()
    spreads[3].last()
    student.last()
    student.end()
    prepare()
    process(0, 0)
    mail.got(block(0, 2, 0), z_up_on)
    start_y(2, 0)
    mail.got(block(0, 2, 1), z_down_on)
    start_y(2, 1)
    for spread in spreads:
        spread.end()
    for step in range(1, n_row):
        mail.got(feat_in.at[(row + n_row - step) % n_row], feat_mail[step - 1])
    proj_width = proj.shape[2]

    def project(source, carry):
        total = jnp.zeros((proj_width, per_device), jnp.float32)
        for features in range(n_row):
            z, x = features // ring, features % ring
            total += lax.dot_general(
                proj[x * 2 + source % 2, source // 2 * ring + z],
                feat_in[features],
                nt_dims,
                preferred_element_type=jnp.float32,
            )
        embed[pl.ds(pl.multiple_of(source * proj_width, 8), proj_width), :] = total
        return carry

    lax.fori_loop(0, n_col, project, 0)
    raw_teacher = embed[...]
    scale = lax.rsqrt(jnp.sum(raw_teacher * raw_teacher, axis=0, keepdims=True) + norm_eps)
    img_t[slot] = (raw_teacher * scale).T.astype(jnp.bfloat16)
    teacher = AlongX(mail, place, img_t)
    teacher.start()
    forward_y(-1)
    teacher.forward()
    pair = ring // 2
    mail.got(last_rows(-1, 0, ring), last_up)
    last_up = mail.push(last_rows(-1, 0, pair), last_rows(-1, 0, pair), place.to_z(1))
    mail.got(last_rows(1, 0, ring), last_down)
    last_down = mail.push(last_rows(1, pair, pair), last_rows(1, pair, pair), place.to_z(-1))
    forward_y(1)
    end_y(-1)
    process(0, -1)
    teacher.last()
    end_y(1)
    process(0, 1)
    forward_y(2)
    teacher.end()
    process(1, 0)
    process(1, -1)
    process(1, 1)
    end_y(2)
    mail.got(last_rows(2, 0, pair), last_up)
    mail.got(last_rows(2, pair, pair), last_down)
    process(0, 2)
    process(1, 2)

    for source in range(n_col):
        rows = slice(source * per_device, (source + 1) * per_device)
        found = []
        for kind in range(2):
            high_all = row_high[kind, rows].T
            high = jnp.max(high_all, axis=0, keepdims=True)
            total = jnp.sum(
                row_total[kind, rows].T * jnp.exp2(high_all - high), axis=0, keepdims=True
            )
            found += [high, total]
        row_stats[source] = jnp.concatenate(
            found + [jnp.zeros((4, per_device), jnp.float32)], axis=0
        )
    row_mail = [
        mail.push(
            row_stats.at[(slot + step) % n_col], row_landed.at[slot], place.to_slot(step)
        )
        for step in range(1, n_col)
    ]
    row_landed[slot] = row_stats[slot]

    def merge(parts):
        found = []
        for kind in range(2):
            high = jnp.max(parts[:, 2 * kind], axis=0, keepdims=True)
            total = jnp.sum(
                parts[:, 2 * kind + 1] * jnp.exp2(parts[:, 2 * kind] - high),
                axis=0,
                keepdims=True,
            )
            found.append(high + jnp.log2(total) + float(kind))
        return jnp.concatenate(found + [jnp.zeros((6, per_device), jnp.float32)], axis=0)

    pairs_of_steps = [(dy, dz) for dy in range(ring) for dz in range(ring) if dy or dz]
    for dy, dz in pairs_of_steps:
        mail.got(col_landed.at[place.along_y(-dy), place.along_z(-dz)], col_mail[dy, dz])
    col_lse[own_y, own_z] = merge(col_landed[...].reshape(n_row, 8, per_device))
    own_lse = col_lse.at[own_y, own_z]
    col_back = {
        (dy, dz): mail.push(own_lse, own_lse, place.to_text(dy, dz)) for dy, dz in pairs_of_steps
    }
    for step in range(1, n_col):
        mail.got(row_landed.at[(slot + n_col - step) % n_col], row_mail[step - 1])
    row_lse[slot] = merge(row_landed[...])
    row_back = [
        mail.push(row_lse.at[slot], row_lse.at[slot], place.to_slot(step))
        for step in range(1, n_col)
    ]
    for step in range(1, n_col):
        mail.got(row_lse.at[(slot + n_col - step) % n_col], row_back[step - 1])
    for source in range(n_col):
        rows = slice(source * per_device, (source + 1) * per_device)
        for kind in range(2):
            wide = row_lse[source, kind : kind + 1, :]
            row_tiles[kind, rows] = jnp.broadcast_to(wide, (per_device, per_device)).T
    for dy, dz in pairs_of_steps:
        mail.got(col_lse.at[place.along_y(-dy), place.along_z(-dz)], col_back[dy, dz])

    over = {}
    across = {}

    def weigh(step):
        target = place.along_x(step)
        rows = pl.ds(pl.multiple_of(target * image_rows, image_rows), image_rows)
        partial_grad[target] = jnp.zeros(partial_grad.shape[1:], jnp.float32)

        def texts(index, carry):
            parts = []
            for y in range(ring):
                lane = slice(y * per_device, (y + 1) * per_device)
                student_scores = scores[0, index, rows, lane]
                teacher_scores = scores[1, index, rows, lane]
                first_id = ((index * ring + place.x) * n_col + y * 2 + core) * per_device
                matched = jnp.where(offsets[rows] == first_id, 1.0, 0.0)
                weights = (
                    jnp.exp2(student_scores - row_tiles[0, rows])
                    + jnp.exp2(student_scores - col_lse[y, index, 0:1, :])
                    - jnp.exp2(teacher_scores - row_tiles[1, rows])
                    - jnp.exp2(teacher_scores - col_lse[y, index, 1:2, :])
                    - matched
                )
                parts.append(weights.astype(jnp.bfloat16))
            product = jnp.dot(
                jnp.concatenate(parts, axis=1),
                text_student(index),
                preferred_element_type=jnp.float32,
            )
            partial_grad[target] += product.reshape(2, per_device, width)
            return carry

        lax.fori_loop(0, ring, texts, 0)
        over[step] = mail.push(
            partial_grad.at[target, other], from_core.at[target], place.sibling()
        )

    def pass_over(step):
        target = place.along_x(step)
        mail.got(from_core.at[target], over[step])
        total = partial_grad[target, core] + from_core[target]
        if step:
            leaving[step - 1] = total.astype(jnp.bfloat16)
            across[step] = mail.push(
                leaving.at[step - 1], arriving.at[step - 1], place.to_x(step)
            )
        return total

    weigh(2)
    weigh(1)
    pass_over(2)
    weigh(3)
    pass_over(1)
    weigh(0)
    pass_over(3)
    embed_grad = pass_over(0)
    for step in (2, 1, 3):
        mail.got(arriving.at[step - 1], across[step])
        embed_grad = embed_grad + arriving[step - 1].astype(jnp.float32)
    embed_grad = logit_scale * embed_grad
    raw_student = raw_ref[...]
    scale = lax.rsqrt(jnp.sum(raw_student * raw_student, axis=1, keepdims=True) + norm_eps)
    student_unit = raw_student * scale
    inner_term = jnp.sum(student_unit * embed_grad, axis=1, keepdims=True)
    grad_embed = (embed_grad - student_unit * inner_term) * scale
    embed_out[...] = grad_embed
    grads[...] = grad_embed.astype(jnp.bfloat16)
    ticket = mail.push(grads, grads_sibling, place.sibling())

    pieces, kinds, size = summed.shape[:3]
    for kind in range(kinds):
        start = pl.multiple_of(core * share + kind * size, size)
        product = lax.dot_general(
            si_ref[:, pl.ds(start, size)],
            grads[...],
            tn_dims,
            preferred_element_type=jnp.float32,
        )
        for lane in range(pieces):
            summed[lane, kind] = product[:, lane * size : (lane + 1) * size]
    mail.got(si_sibling, si_mail)
    mail.got(grads_sibling, ticket)
    for kind in range(kinds):
        product = lax.dot_general(
            si_sibling[:, kind * size : (kind + 1) * size],
            grads_sibling[...],
            tn_dims,
            preferred_element_type=jnp.float32,
        )
        for lane in range(pieces):
            total = summed[lane, kind] + product[:, lane * size : (lane + 1) * size]
            summed[lane, kind] = total
            first_out[lane, kind] = total.astype(jnp.bfloat16)

    along_x = (place.x, place.along_x, place.to_x)
    along_y = (place.y, place.along_y, place.to_y)
    families = ((pl.ds(0, 2), along_y, along_x), (pl.ds(2, 1), along_x, along_y))
    quarter, tile = size // ring, size // n_row
    steps = (2, 1, 3)

    def rows_of(position, count):
        return pl.ds(pl.multiple_of(position * count, count), count)

    tickets = {}
    for index, (chosen, (own, at, to), _) in enumerate(families):
        for step in steps:
            tickets[index, step] = mail.push(
                first_out.at[at(step), chosen], first_in.at[step - 1, chosen], to(step)
            )
    for index, (chosen, (own, at, to), (own_next, at_next, to_next)) in enumerate(families):
        total = summed[own, chosen]
        for step in steps:
            mail.got(first_in.at[step - 1, chosen], tickets[index, step])
            total = total + first_in[step - 1, chosen].astype(jnp.float32)
        second[chosen] = total
        second_out[chosen] = total.astype(jnp.bfloat16)
        for step in steps:
            tickets[index, step] = mail.push(
                second_out.at[chosen, rows_of(at_next(step), quarter)],
                second_in.at[step - 1, chosen],
                to_next(step),
            )
    for index, (chosen, _, (own, at, to)) in enumerate(families):
        total = second[chosen, rows_of(own, quarter)]
        for step in steps:
            mail.got(second_in.at[step - 1, chosen], tickets[index, step])
            total = total + second_in[step - 1, chosen].astype(jnp.float32)
        third[chosen] = total
    for step in steps:
        tickets[step] = mail.push(
            third.at[:, rows_of(place.along_z(step), tile)], third_in.at[step - 1], place.to_z(step)
        )
    total = third[:, rows_of(place.z, tile)]
    for step in steps:
        mail.got(third_in.at[step - 1], tickets[step])
        total = total + third_in[step - 1]
    group = lax.axis_index("group")

    def group_tile(side, step):
        return group_sums.at[side, :, rows_of(place.along_z(step), tile)]

    group_tile(group, 0)[...] = total
    own_tile = group_tile(group, 0)
    for step in steps:
        tickets[0, step] = mail.push(own_tile, own_tile, place.to_z(step))
    for step in range(ring):
        tickets[1, step] = mail.push(own_tile, own_tile, place.across(step))
    for step in steps:
        mail.got(group_tile(group, -step), tickets[0, step])
    for step in range(ring):
        mail.got(group_tile(1 - group, -step), tickets[1, step])
    total = (group_sums[0] + group_sums[1]).astype(jnp.bfloat16)

    for index, (chosen, (own1, at1, to1), (own2, at2, to2)) in enumerate(families):
        mine = gathered.at[core, own1, chosen, rows_of(own2, quarter)]
        mine[...] = total[chosen.start : chosen.start + chosen.size]
        for step in steps:
            tickets[index, step] = mail.push(mine, mine, to2(step))
    back = {}
    for index, (chosen, (own1, at1, to1), (own2, at2, to2)) in enumerate(families):
        for step in steps:
            mail.got(
                gathered.at[core, own1, chosen, rows_of(at2(-step), quarter)],
                tickets[index, step],
            )
        mine = gathered.at[core, own1, chosen]
        for step in steps:
            tickets[index, step] = mail.push(mine, mine, to1(step))
        back[index, 0] = mail.push(mine, mine, place.sibling())
    for step in (1, 3, 2):
        for index, (chosen, (own1, at1, to1), _) in enumerate(families):
            theirs = gathered.at[core, at1(-step), chosen]
            mail.got(theirs, tickets[index, step])
            back[index, step] = mail.push(theirs, theirs, place.sibling())

    for step in (0, 1, 3, 2):
        for index, (chosen, (own1, at1, to1), _) in enumerate(families):
            mail.got(gathered.at[other, at1(-step), chosen], back[index, step])
    mail.finish()


def body(
    student_image,
    student_proj,
    student_text,
    teacher_image,
    teacher_proj,
    teacher_text,
    assignment,
    pair_ids,
):
    per_device, width = student_text.shape
    teacher_width = teacher_text.shape[1]
    student_width = student_image.shape[1]
    features, proj_width = teacher_proj.shape
    size = 128
    kinds = student_width // (2 * size)
    pieces = width // size
    bf16, f32, i32 = jnp.bfloat16, jnp.float32, jnp.int32
    tile = (8, per_device)
    chunk = ring * per_device
    images = n_col * per_device
    hbm = pl.BlockSpec(memory_space=pl.ANY)
    vmem = pl.BlockSpec(memory_space=pltpu.VMEM)
    copies = 236
    grad_embed, gathered = pl.pallas_call(
        step_kernel,
        out_shape=(
            jax.ShapeDtypeStruct((per_device, width), f32),
            jax.ShapeDtypeStruct((2, pieces, kinds, size, size), bf16),
        ),
        in_specs=[hbm] * 8,
        out_specs=[vmem] * 2,
        scratch_shapes=[
            pltpu.VMEM(student_image.shape, bf16),
            pltpu.VMEM(student_proj.shape, bf16),
            pltpu.VMEM(student_text.shape, bf16),
            pltpu.VMEM((features, n_row * per_device), bf16),
            pltpu.VMEM(teacher_text.shape, bf16),
            pltpu.VMEM((ring, ring, per_device, teacher_width + width), bf16),
            pltpu.VMEM((n_col, per_device, width), bf16),
            pltpu.VMEM((n_col, per_device, teacher_width), bf16),
            pltpu.VMEM((n_col, 1, per_device), i32),
            pltpu.VMEM((per_device, width), f32),
            pltpu.VMEM((n_row, 1, per_device), i32),
            pltpu.VMEM((n_row, per_device, features), bf16),
            pltpu.VMEM((n_row, per_device, features), bf16),
            pltpu.VMEM((n_col, n_row, proj_width, features), bf16),
            pltpu.VMEM((teacher_width, per_device), f32),
            pltpu.VMEM((2, ring, images, chunk), f32),
            pltpu.VMEM((2, images, per_device), f32),
            pltpu.VMEM((2, images, per_device), f32),
            pltpu.VMEM((8, chunk), f32),
            pltpu.VMEM((8, chunk), f32),
            pltpu.VMEM((n_col,) + tile, f32),
            pltpu.VMEM((n_col,) + tile, f32),
            pltpu.VMEM((n_col,) + tile, f32),
            pltpu.VMEM((ring, ring) + tile, f32),
            pltpu.VMEM((ring, ring) + tile, f32),
            pltpu.VMEM((ring, ring) + tile, f32),
            pltpu.VMEM((2, images, per_device), f32),
            pltpu.VMEM((images, per_device), i32),
            pltpu.VMEM((ring, 2, per_device, width), f32),
            pltpu.VMEM((ring, per_device, width), f32),
            pltpu.VMEM((ring - 1, per_device, width), bf16),
            pltpu.VMEM((ring - 1, per_device, width), bf16),
            pltpu.VMEM((per_device, student_width // 2), bf16),
            pltpu.VMEM((per_device, width), bf16),
            pltpu.VMEM((per_device, width), bf16),
            pltpu.VMEM((pieces, kinds, size, size), f32),
            pltpu.VMEM((pieces, kinds, size, size), bf16),
            pltpu.VMEM((ring - 1, kinds, size, size), bf16),
            pltpu.VMEM((kinds, size, size), f32),
            pltpu.VMEM((kinds, size, size), bf16),
            pltpu.VMEM((ring - 1, kinds, size // 4, size), bf16),
            pltpu.VMEM((kinds, size // 4, size), f32),
            pltpu.VMEM((ring - 1, kinds, 8, size), f32),
            pltpu.VMEM((2, kinds, size // 4, size), f32),
            pltpu.SemaphoreType.DMA((8,)),
            pltpu.SemaphoreType.DMA((96,)),
            pltpu.SemaphoreType.DMA((copies,)),
        ],
        compiler_params=pltpu.CompilerParams(
            collective_id=0, has_side_effects=True, vmem_limit_bytes=60 * 1024 * 1024
        ),
    )(
        student_image,
        student_proj,
        student_text,
        teacher_image.T,
        teacher_proj.T,
        teacher_text,
        assignment,
        pair_ids,
    )
    grad_proj = gathered.transpose(0, 2, 3, 1, 4).reshape(student_width, width)
    return grad_embed, grad_proj.astype(f32)


def solution(mesh):
    placed = (
        P(("group", "row", "col"), None),
        P(),
        P(("group", "row", "col"), None),
        P(("group", "col"), "row"),
        P("row", "col"),
        P(("group", "row", "col"), None),
        P("group", ("row", "col")),
        P("group", ("row", "col")),
    )
    return jax.shard_map(
        body,
        mesh=mesh,
        in_specs=placed,
        out_specs=(P(("group", "row", "col"), None), P()),
        check_vma=False,
    )
```

```python
import math

import jax
import jax.numpy as jnp
from jax import lax
from jax.experimental import pallas as pl
from jax.experimental.pallas import tpu as pltpu
from jax.sharding import PartitionSpec as P

logit_scale = 100.0
score_scale = logit_scale * math.log2(math.e)
lowest = -1e30
norm_eps = 1e-06
MESH = pl.DeviceIdType.MESH
ring = 4
n_row = 16
n_col = 8
nt_dims = (((1,), (1,)), ((), ()))
tn_dims = (((0,), (0,)), ((), ()))


def unit_rows(values):
    return values * lax.rsqrt(jnp.sum(values * values, axis=1, keepdims=True) + norm_eps)


class Place:
    def __init__(self):
        self.row = lax.axis_index("row")
        self.col = lax.axis_index("col")
        self.z, self.x = self.row // ring, self.row % ring
        self.y, self.core = self.col // 2, self.col % 2
        self.slot = self.x * 2 + self.core

    def along_x(self, step):
        return (self.x + step + ring) % ring

    def along_y(self, step):
        return (self.y + step + ring) % ring

    def along_z(self, step):
        return (self.z + step + ring) % ring

    def to_x(self, step):
        return {"row": self.z * ring + self.along_x(step)}

    def to_z(self, step):
        return {"row": self.along_z(step) * ring + self.x}

    def to_y(self, step):
        return {"col": self.along_y(step) * 2 + self.core}

    def to_slot(self, step):
        slot = (self.slot + step) % n_col
        return {"row": self.z * ring + slot // 2, "col": self.y * 2 + slot % 2}

    def to_text(self, dy, dz):
        return {
            "row": self.along_z(dz) * ring + self.x,
            "col": self.along_y(dy) * 2 + self.core,
        }

    def across(self, step):
        return {
            "group": 1 - lax.axis_index("group"),
            "row": self.along_z(step) * ring + self.x,
        }

    def sibling(self):
        return {"col": self.y * 2 + 1 - self.core}


class Mail:
    def __init__(self, send_sem, recv_sem):
        self.send_sem, self.recv_sem = send_sem, recv_sem
        self.used = 0
        self.sent = {}

    def push(self, src, dst, device):
        index = self.used
        self.used += 1
        turn = index % self.send_sem.shape[0]
        if turn in self.sent:
            self.sent[turn].wait_send()
        copy = pltpu.make_async_remote_copy(
            src_ref=src,
            dst_ref=dst,
            send_sem=self.send_sem.at[turn],
            recv_sem=self.recv_sem.at[index],
            device_id=device,
            device_id_type=MESH,
        )
        copy.start()
        self.sent[turn] = copy
        return index, device

    def got(self, slot, ticket):
        index, device = ticket
        pltpu.make_async_remote_copy(
            src_ref=slot,
            dst_ref=slot,
            send_sem=self.send_sem.at[0],
            recv_sem=self.recv_sem.at[index],
            device_id=device,
            device_id_type=MESH,
        ).wait_recv()

    def finish(self):
        for copy in self.sent.values():
            copy.wait_send()


def all_peers(place):
    return (
        [{"row": (place.row + step) % n_row} for step in range(1, n_row)]
        + [place.to_text(dy, dz) for dy in range(1, ring) for dz in range(ring)]
        + [
            {
                "row": place.z * ring + place.along_x(step),
                "col": place.y * 2 + 1 - place.core,
            }
            for step in range(ring)
        ]
        + [place.across(step) for step in range(ring)]
    )


class AlongX:
    def __init__(self, mail, place, ref, first=0, count=None):
        self.mail, self.place, self.ref = mail, place, ref
        self.first, self.count = first, count or ref.shape[1]
        self.half = self.count // 2

    def whole(self, index):
        return self.ref.at[index, pl.ds(self.first, self.count)]

    def block(self, step, core):
        return self.place.along_x(step) * 2 + core

    def lower(self, index):
        return self.ref.at[index, pl.ds(self.first, self.half)]

    def upper(self, index):
        return self.ref.at[index, pl.ds(self.first + self.half, self.half)]

    def start(self):
        place, mail = self.place, self.mail
        own = self.whole(place.slot)
        self.up = mail.push(own, own, place.to_x(1))
        self.down = mail.push(own, own, place.to_x(-1))
        self.over = [mail.push(own, own, place.sibling())]

    def forward(self):
        place, mail = self.place, self.mail
        below = self.block(-1, place.core)
        mail.got(self.whole(below), self.up)
        self.up_half = mail.push(self.lower(below), self.lower(below), place.to_x(1))
        self.over.append(mail.push(self.whole(below), self.whole(below), place.sibling()))
        above = self.block(1, place.core)
        mail.got(self.whole(above), self.down)
        self.down_half = mail.push(self.upper(above), self.upper(above), place.to_x(-1))
        self.over.append(mail.push(self.whole(above), self.whole(above), place.sibling()))

    def last(self):
        place, mail = self.place, self.mail
        far = self.block(2, place.core)
        mail.got(self.lower(far), self.up_half)
        self.over.append(mail.push(self.lower(far), self.lower(far), place.sibling()))
        mail.got(self.upper(far), self.down_half)
        self.over.append(mail.push(self.upper(far), self.upper(far), place.sibling()))

    def end(self):
        place, mail = self.place, self.mail
        other = 1 - place.core
        mail.got(self.whole(self.block(0, other)), self.over[0])
        mail.got(self.whole(self.block(-1, other)), self.over[1])
        mail.got(self.whole(self.block(1, other)), self.over[2])
        far = self.block(2, other)
        mail.got(self.lower(far), self.over[3])
        mail.got(self.upper(far), self.over[4])


def step_kernel(
    si_hbm,
    sp_hbm,
    st_hbm,
    ti_hbm,
    pt_hbm,
    tt_hbm,
    order_hbm,
    pair_hbm,
    embed_out,
    gathered,
    si_ref,
    sp_ref,
    st_ref,
    ti_ref,
    tt_ref,
    text,
    img_s,
    img_t,
    pairs,
    raw_ref,
    orders,
    feat_out,
    feat_in,
    proj,
    embed,
    scores,
    row_high,
    row_total,
    col_high,
    col_total,
    row_stats,
    row_landed,
    row_lse,
    col_stats,
    col_landed,
    col_lse,
    row_tiles,
    offsets,
    partial_grad,
    from_core,
    leaving,
    arriving,
    si_sibling,
    grads,
    grads_sibling,
    summed,
    first_out,
    first_in,
    second,
    second_out,
    second_in,
    third,
    third_in,
    group_sums,
    load_sem,
    send_sem,
    recv_sem,
):
    place = Place()
    mail = Mail(send_sem, recv_sem)
    row, col, core, slot = place.row, place.col, place.core, place.slot
    other = 1 - core
    per_device, width = st_ref.shape
    teacher_width = tt_ref.shape[1]
    first_part, second_part = 3 * per_device // 8, per_device // 2
    share = si_ref.shape[1] // 2

    barrier = pltpu.get_barrier_semaphore()
    peers = all_peers(place)
    for device in peers:
        pl.semaphore_signal(barrier, inc=1, device_id=device, device_id_type=MESH)
    loads = []
    for source, target in (
        (order_hbm, orders.at[row]),
        (pt_hbm, proj.at[slot, place.y * ring + place.z]),
        (pair_hbm, pairs.at[slot]),
        (st_hbm, st_ref),
        (tt_hbm, tt_ref),
        (si_hbm, si_ref),
        (sp_hbm, sp_ref),
        (ti_hbm, ti_ref),
    ):
        copy = pltpu.make_async_copy(source, target, load_sem.at[len(loads)])
        copy.start()
        loads.append(copy)
    for copy in loads[:5]:
        copy.wait()
    own_y, own_z = place.y, place.z
    text[own_z, own_y, :, :teacher_width] = unit_rows(tt_ref[...].astype(jnp.float32)).astype(
        jnp.bfloat16
    )
    text[own_z, own_y, :, teacher_width:] = unit_rows(st_ref[...].astype(jnp.float32)).astype(
        jnp.bfloat16
    )
    pl.semaphore_wait(barrier, len(peers))

    own_proj = proj.at[slot, place.y * ring + place.z]
    proj_z = [mail.push(own_proj, own_proj, place.to_z(step)) for step in (1, 3, 2)]

    def block(dy, dz, part):
        start, count = ((0, first_part), (first_part, second_part))[part]
        return text.at[place.along_z(dz), place.along_y(dy), pl.ds(start, count)]

    def last_rows(dz, first_y, count):
        return text.at[
            place.along_z(dz),
            pl.ds(first_y, count),
            pl.ds(first_part + second_part, per_device - first_part - second_part),
        ]

    z_up, z_down, y_up, y_down, y_on = {}, {}, {}, {}, {}

    def start_z(part):
        z_up[part] = mail.push(block(0, 0, part), block(0, 0, part), place.to_z(1))
        z_down[part] = mail.push(block(0, 0, part), block(0, 0, part), place.to_z(-1))

    def start_y(dz, part):
        y_up[dz, part] = mail.push(block(0, dz, part), block(0, dz, part), place.to_y(1))
        y_down[dz, part] = mail.push(block(0, dz, part), block(0, dz, part), place.to_y(-1))

    def forward_y(dz):
        mail.got(block(-1, dz, 0), y_up[dz, 0])
        y_on[dz, 0] = mail.push(block(-1, dz, 0), block(-1, dz, 0), place.to_y(1))
        mail.got(block(1, dz, 1), y_down[dz, 1])
        y_on[dz, 1] = mail.push(block(1, dz, 1), block(1, dz, 1), place.to_y(-1))

    start_z(0)
    own_last = last_rows(0, own_y, 1)
    last_y = [mail.push(own_last, own_last, place.to_y(step)) for step in (1, 3, 2)]
    start_y(0, 0)
    own_order = orders.at[row]
    order_mail = [
        mail.push(own_order, own_order, {"row": (row + step) % n_row}) for step in range(1, n_row)
    ]
    loads[5].wait()
    loads[6].wait()
    si_mail = mail.push(
        si_ref.at[:, pl.ds(pl.multiple_of(other * share, share), share)],
        si_sibling,
        place.sibling(),
    )
    raw_student = jnp.dot(si_ref[...], sp_ref[...], preferred_element_type=jnp.float32)
    raw_ref[...] = raw_student
    img_s[slot] = unit_rows(raw_student).astype(jnp.bfloat16)
    for step, ticket in zip((1, 3, 2), proj_z):
        mail.got(proj.at[slot, place.y * ring + place.along_z(-step)], ticket)

    def proj_rows(step, start=0, count=ring):
        return proj.at[slot, pl.ds(place.along_y(step) * ring + start, count)]

    def proj_spread(step):
        spread = AlongX(mail, place, proj, place.along_y(step) * ring, ring)
        spread.start()
        return spread

    proj_up = mail.push(proj_rows(0), proj_rows(0), place.to_y(1))
    proj_down = mail.push(proj_rows(0), proj_rows(0), place.to_y(-1))
    spreads = [proj_spread(0)]
    start_z(1)
    start_y(0, 1)
    student = AlongX(mail, place, img_s)
    student.start()
    own_pairs = pairs.at[slot]
    pair_mail = [mail.push(own_pairs, own_pairs, place.to_slot(step)) for step in range(1, n_col)]

    image_rows = 2 * per_device
    chunk = ring * per_device
    col_mail = {}

    def end_y(dz):
        mail.got(block(-1, dz, 1), y_up[dz, 1])
        mail.got(block(1, dz, 0), y_down[dz, 0])
        mail.got(block(2, dz, 0), y_on[dz, 0])
        mail.got(block(2, dz, 1), y_on[dz, 1])

    def prepare():
        end_y(0)
        for step in range(1, n_col):
            mail.got(pairs.at[(slot + n_col - step) % n_col], pair_mail[step - 1])
        lane_ids = lax.broadcasted_iota(jnp.int32, (per_device, per_device), 1)
        for source in range(n_col):
            wide = jnp.broadcast_to(pairs[source].astype(jnp.float32), (per_device, per_device)).T
            offsets[source * per_device : (source + 1) * per_device] = (
                wide.astype(jnp.int32) - lane_ids
            )
        row_high[...] = jnp.full(row_high.shape, lowest, jnp.float32)
        row_total[...] = jnp.zeros(row_total.shape, jnp.float32)
        col_stats[...] = jnp.zeros(col_stats.shape, jnp.float32)

    def text_student(index):
        return text[index, :, :, teacher_width:].reshape(chunk, width)

    def text_teacher(index):
        return text[index, :, :, :teacher_width].reshape(chunk, teacher_width)

    def process(kind, dz):
        index = place.along_z(dz)
        col_high[...] = jnp.full(col_high.shape, lowest, jnp.float32)
        col_total[...] = jnp.zeros(col_total.shape, jnp.float32)

        def images(step, carry):
            rows = pl.ds(pl.multiple_of(step * image_rows, image_rows), image_rows)
            if kind == 0:
                left = img_s[pl.ds(2 * step, 2)].reshape(image_rows, width)
                right = text_student(index)
            else:
                left = img_t[pl.ds(2 * step, 2)].reshape(image_rows, teacher_width)
                right = text_teacher(index)
            values = score_scale * lax.dot_general(
                left, right, nt_dims, preferred_element_type=jnp.float32
            )
            scores[kind, index, rows] = values
            tiles = [values[:, start : start + per_device] for start in range(0, chunk, per_device)]
            before = row_high[kind, rows]
            high = before
            for tile in tiles:
                high = jnp.maximum(high, tile)
            total = row_total[kind, rows] * jnp.exp2(before - high)
            for tile in tiles:
                total = total + jnp.exp2(tile - high)
            row_high[kind, rows] = high
            row_total[kind, rows] = total
            stacked = values.reshape(image_rows // 8, 8, chunk)
            before = col_high[...]
            high = jnp.maximum(before, jnp.max(stacked, axis=0))
            total = col_total[...] * jnp.exp2(before - high)
            col_total[...] = total + jnp.sum(jnp.exp2(stacked - high[None]), axis=0)
            col_high[...] = high
            return carry

        lax.fori_loop(0, ring, images, 0)
        high = jnp.max(col_high[...], axis=0, keepdims=True)
        total = jnp.sum(col_total[...] * jnp.exp2(col_high[...] - high), axis=0, keepdims=True)
        for y in range(ring):
            lane = slice(y * per_device, (y + 1) * per_device)
            col_stats[index, y, 2 * kind : 2 * kind + 1] = high[:, lane]
            col_stats[index, y, 2 * kind + 1 : 2 * kind + 2] = total[:, lane]
        if kind == 1:
            for dy in range(ring):
                y = place.along_y(dy)
                if dy or dz:
                    col_mail[dy, dz % ring] = mail.push(
                        col_stats.at[index, y],
                        col_landed.at[own_y, own_z],
                        place.to_text(dy, dz),
                    )
                else:
                    col_landed[own_y, own_z] = col_stats[index, y]

    loads[7].wait()
    for step in range(1, n_row):
        mail.got(orders.at[(row + n_row - step) % n_row], order_mail[step - 1])
    lanes = lax.broadcasted_iota(jnp.int32, (per_device, 2 * per_device), 1).astype(jnp.float32)

    def pick(target, carry):
        wanted = (orders[target] - col * (n_row * per_device)).astype(jnp.float32)
        wanted = jnp.broadcast_to(wanted, (per_device, per_device)).T
        wanted = jnp.concatenate([wanted, wanted], axis=1)
        total = jnp.zeros((per_device, ti_ref.shape[0]), jnp.float32)
        for start in range(0, n_row * per_device, 2 * per_device):
            chosen = jnp.where(wanted == lanes + float(start), 1.0, 0.0).astype(jnp.bfloat16)
            total += lax.dot_general(
                chosen,
                ti_ref[:, start : start + 2 * per_device],
                nt_dims,
                preferred_element_type=jnp.float32,
            )
        feat_out[target] = total.astype(jnp.bfloat16)
        return carry

    half_rows = ring // 2
    lower, upper = (0, half_rows), (half_rows, half_rows)
    lax.fori_loop(0, n_row // 2, pick, 0)
    mail.got(proj_rows(-1), proj_up)
    proj_up = mail.push(proj_rows(-1, *lower), proj_rows(-1, *lower), place.to_y(1))
    spreads.append(proj_spread(-1))
    mail.got(proj_rows(1), proj_down)
    proj_down = mail.push(proj_rows(1, *upper), proj_rows(1, *upper), place.to_y(-1))
    spreads.append(proj_spread(1))
    spreads[0].forward()
    lax.fori_loop(n_row // 2, n_row, pick, 0)
    feat_mail = []
    for step in range(1, n_row):
        target = (row + step) % n_row
        feat_mail.append(mail.push(feat_out.at[target], feat_in.at[row], {"row": target}))
    feat_in[row] = feat_out[row]
    mail.got(proj_rows(2, *lower), proj_up)
    mail.got(proj_rows(2, *upper), proj_down)
    spreads.append(proj_spread(2))

    mail.got(block(0, -1, 0), z_up[0])
    z_up_on = mail.push(block(0, -1, 0), block(0, -1, 0), place.to_z(1))
    start_y(-1, 0)
    mail.got(block(0, 1, 0), z_down[0])
    start_y(1, 0)
    forward_y(0)
    spreads[0].last()
    spreads[1].forward()
    spreads[2].forward()
    mail.got(block(0, 1, 1), z_down[1])
    z_down_on = mail.push(block(0, 1, 1), block(0, 1, 1), place.to_z(-1))
    start_y(1, 1)
    mail.got(block(0, -1, 1), z_up[1])
    start_y(-1, 1)
    for step, ticket in zip((1, 3, 2), last_y):
        mail.got(last_rows(0, place.along_y(-step), 1), ticket)
    last_up = mail.push(last_rows(0, 0, ring), last_rows(0, 0, ring), place.to_z(1))
    last_down = mail.push(last_rows(0, 0, ring), last_rows(0, 0, ring), place.to_z(-1))
    spreads[1].last()
    spreads[2].last()
    spreads[3].forward()
    student.forward()
    spreads[3].last()
    student.last()
    student.end()
    prepare()
    process(0, 0)
    mail.got(block(0, 2, 0), z_up_on)
    start_y(2, 0)
    mail.got(block(0, 2, 1), z_down_on)
    start_y(2, 1)
    for spread in spreads:
        spread.end()
    for step in range(1, n_row):
        mail.got(feat_in.at[(row + n_row - step) % n_row], feat_mail[step - 1])
    proj_width = proj.shape[2]

    def project(source, carry):
        total = jnp.zeros((proj_width, per_device), jnp.float32)
        for features in range(n_row):
            z, x = features // ring, features % ring
            total += lax.dot_general(
                proj[x * 2 + source % 2, source // 2 * ring + z],
                feat_in[features],
                nt_dims,
                preferred_element_type=jnp.float32,
            )
        embed[pl.ds(pl.multiple_of(source * proj_width, 8), proj_width), :] = total
        return carry

    lax.fori_loop(0, n_col, project, 0)
    raw_teacher = embed[...]
    scale = lax.rsqrt(jnp.sum(raw_teacher * raw_teacher, axis=0, keepdims=True) + norm_eps)
    img_t[slot] = (raw_teacher * scale).T.astype(jnp.bfloat16)
    teacher = AlongX(mail, place, img_t)
    teacher.start()
    forward_y(-1)
    teacher.forward()
    pair = ring // 2
    mail.got(last_rows(-1, 0, ring), last_up)
    last_up = mail.push(last_rows(-1, 0, pair), last_rows(-1, 0, pair), place.to_z(1))
    mail.got(last_rows(1, 0, ring), last_down)
    last_down = mail.push(last_rows(1, pair, pair), last_rows(1, pair, pair), place.to_z(-1))
    forward_y(1)
    end_y(-1)
    process(0, -1)
    teacher.last()
    end_y(1)
    process(0, 1)
    forward_y(2)
    teacher.end()
    process(1, 0)
    process(1, -1)
    process(1, 1)
    end_y(2)
    mail.got(last_rows(2, 0, pair), last_up)
    mail.got(last_rows(2, pair, pair), last_down)
    process(0, 2)
    process(1, 2)

    for source in range(n_col):
        rows = slice(source * per_device, (source + 1) * per_device)
        found = []
        for kind in range(2):
            high_all = row_high[kind, rows].T
            high = jnp.max(high_all, axis=0, keepdims=True)
            total = jnp.sum(
                row_total[kind, rows].T * jnp.exp2(high_all - high), axis=0, keepdims=True
            )
            found += [high, total]
        row_stats[source] = jnp.concatenate(
            found + [jnp.zeros((4, per_device), jnp.float32)], axis=0
        )
    row_mail = [
        mail.push(
            row_stats.at[(slot + step) % n_col], row_landed.at[slot], place.to_slot(step)
        )
        for step in range(1, n_col)
    ]
    row_landed[slot] = row_stats[slot]

    def merge(parts):
        found = []
        for kind in range(2):
            high = jnp.max(parts[:, 2 * kind], axis=0, keepdims=True)
            total = jnp.sum(
                parts[:, 2 * kind + 1] * jnp.exp2(parts[:, 2 * kind] - high),
                axis=0,
                keepdims=True,
            )
            found.append(high + jnp.log2(total) + float(kind))
        return jnp.concatenate(found + [jnp.zeros((6, per_device), jnp.float32)], axis=0)

    pairs_of_steps = [(dy, dz) for dy in range(ring) for dz in range(ring) if dy or dz]
    for dy, dz in pairs_of_steps:
        mail.got(col_landed.at[place.along_y(-dy), place.along_z(-dz)], col_mail[dy, dz])
    col_lse[own_y, own_z] = merge(col_landed[...].reshape(n_row, 8, per_device))
    own_lse = col_lse.at[own_y, own_z]
    col_back = {
        (dy, dz): mail.push(own_lse, own_lse, place.to_text(dy, dz)) for dy, dz in pairs_of_steps
    }
    for step in range(1, n_col):
        mail.got(row_landed.at[(slot + n_col - step) % n_col], row_mail[step - 1])
    row_lse[slot] = merge(row_landed[...])
    row_back = [
        mail.push(row_lse.at[slot], row_lse.at[slot], place.to_slot(step))
        for step in range(1, n_col)
    ]
    for step in range(1, n_col):
        mail.got(row_lse.at[(slot + n_col - step) % n_col], row_back[step - 1])
    for source in range(n_col):
        rows = slice(source * per_device, (source + 1) * per_device)
        for kind in range(2):
            wide = row_lse[source, kind : kind + 1, :]
            row_tiles[kind, rows] = jnp.broadcast_to(wide, (per_device, per_device)).T
    for dy, dz in pairs_of_steps:
        mail.got(col_lse.at[place.along_y(-dy), place.along_z(-dz)], col_back[dy, dz])

    over = {}
    across = {}

    def weigh(step, first=0, last=ring):
        target = place.along_x(step)
        rows = pl.ds(pl.multiple_of(target * image_rows, image_rows), image_rows)
        if first == 0:
            partial_grad[target] = jnp.zeros(partial_grad.shape[1:], jnp.float32)

        def texts(index, carry):
            parts = []
            for y in range(ring):
                lane = slice(y * per_device, (y + 1) * per_device)
                student_scores = scores[0, index, rows, lane]
                teacher_scores = scores[1, index, rows, lane]
                first_id = ((index * ring + place.x) * n_col + y * 2 + core) * per_device
                matched = jnp.where(offsets[rows] == first_id, 1.0, 0.0)
                weights = (
                    jnp.exp2(student_scores - row_tiles[0, rows])
                    + jnp.exp2(student_scores - col_lse[y, index, 0:1, :])
                    - jnp.exp2(teacher_scores - row_tiles[1, rows])
                    - jnp.exp2(teacher_scores - col_lse[y, index, 1:2, :])
                    - matched
                )
                parts.append(weights.astype(jnp.bfloat16))
            product = jnp.dot(
                jnp.concatenate(parts, axis=1),
                text_student(index),
                preferred_element_type=jnp.float32,
            )
            partial_grad[target] += product.reshape(2, per_device, width)
            return carry

        lax.fori_loop(first, last, texts, 0)
        if last == ring:
            over[step] = mail.push(
                partial_grad.at[target, other], from_core.at[target], place.sibling()
            )

    def pass_over(step):
        target = place.along_x(step)
        mail.got(from_core.at[target], over[step])
        total = partial_grad[target, core] + from_core[target]
        if step:
            leaving[step - 1] = total.astype(jnp.bfloat16)
            across[step] = mail.push(
                leaving.at[step - 1], arriving.at[step - 1], place.to_x(step)
            )
        return total

    weigh(2)
    weigh(1)
    pass_over(2)
    weigh(3)
    pass_over(1)
    weigh(0, 0, 3)
    pass_over(3)
    weigh(0, 3, ring)
    embed_grad = pass_over(0)
    for step in (2, 1, 3):
        mail.got(arriving.at[step - 1], across[step])
        embed_grad = embed_grad + arriving[step - 1].astype(jnp.float32)
    embed_grad = logit_scale * embed_grad
    raw_student = raw_ref[...]
    scale = lax.rsqrt(jnp.sum(raw_student * raw_student, axis=1, keepdims=True) + norm_eps)
    student_unit = raw_student * scale
    inner_term = jnp.sum(student_unit * embed_grad, axis=1, keepdims=True)
    grad_embed = (embed_grad - student_unit * inner_term) * scale
    embed_out[...] = grad_embed
    grads[...] = grad_embed.astype(jnp.bfloat16)
    ticket = mail.push(grads, grads_sibling, place.sibling())

    pieces, kinds, size = summed.shape[:3]
    for kind in range(kinds):
        start = pl.multiple_of(core * share + kind * size, size)
        product = lax.dot_general(
            si_ref[:, pl.ds(start, size)],
            grads[...],
            tn_dims,
            preferred_element_type=jnp.float32,
        )
        for lane in range(pieces):
            summed[lane, kind] = product[:, lane * size : (lane + 1) * size]
    mail.got(si_sibling, si_mail)
    mail.got(grads_sibling, ticket)
    for kind in range(kinds):
        product = lax.dot_general(
            si_sibling[:, kind * size : (kind + 1) * size],
            grads_sibling[...],
            tn_dims,
            preferred_element_type=jnp.float32,
        )
        for lane in range(pieces):
            total = summed[lane, kind] + product[:, lane * size : (lane + 1) * size]
            summed[lane, kind] = total
            first_out[lane, kind] = total.astype(jnp.bfloat16)

    along_x = (place.x, place.along_x, place.to_x)
    along_y = (place.y, place.along_y, place.to_y)
    families = ((pl.ds(0, 2), along_y, along_x), (pl.ds(2, 1), along_x, along_y))
    quarter, tile = size // ring, size // n_row
    steps = (2, 1, 3)

    def rows_of(position, count):
        return pl.ds(pl.multiple_of(position * count, count), count)

    tickets = {}
    for index, (chosen, (own, at, to), _) in enumerate(families):
        for step in steps:
            tickets[index, step] = mail.push(
                first_out.at[at(step), chosen], first_in.at[step - 1, chosen], to(step)
            )
    for index, (chosen, (own, at, to), (own_next, at_next, to_next)) in enumerate(families):
        total = summed[own, chosen]
        for step in steps:
            mail.got(first_in.at[step - 1, chosen], tickets[index, step])
            total = total + first_in[step - 1, chosen].astype(jnp.float32)
        second[chosen] = total
        second_out[chosen] = total.astype(jnp.bfloat16)
        for step in steps:
            tickets[index, step] = mail.push(
                second_out.at[chosen, rows_of(at_next(step), quarter)],
                second_in.at[step - 1, chosen],
                to_next(step),
            )
    for index, (chosen, _, (own, at, to)) in enumerate(families):
        total = second[chosen, rows_of(own, quarter)]
        for step in steps:
            mail.got(second_in.at[step - 1, chosen], tickets[index, step])
            total = total + second_in[step - 1, chosen].astype(jnp.float32)
        third[chosen] = total
    for step in steps:
        tickets[step] = mail.push(
            third.at[:, rows_of(place.along_z(step), tile)], third_in.at[step - 1], place.to_z(step)
        )
    total = third[:, rows_of(place.z, tile)]
    for step in steps:
        mail.got(third_in.at[step - 1], tickets[step])
        total = total + third_in[step - 1]
    group = lax.axis_index("group")

    def group_tile(side, step):
        return group_sums.at[side, :, rows_of(place.along_z(step), tile)]

    group_tile(group, 0)[...] = total
    own_tile = group_tile(group, 0)
    for step in steps:
        tickets[0, step] = mail.push(own_tile, own_tile, place.to_z(step))
    for step in range(ring):
        tickets[1, step] = mail.push(own_tile, own_tile, place.across(step))
    for step in steps:
        mail.got(group_tile(group, -step), tickets[0, step])
    for step in range(ring):
        mail.got(group_tile(1 - group, -step), tickets[1, step])
    total = (group_sums[0] + group_sums[1]).astype(jnp.bfloat16)

    for index, (chosen, (own1, at1, to1), (own2, at2, to2)) in enumerate(families):
        mine = gathered.at[core, own1, chosen, rows_of(own2, quarter)]
        mine[...] = total[chosen.start : chosen.start + chosen.size]
        for step in steps:
            tickets[index, step] = mail.push(mine, mine, to2(step))
    back = {}
    for index, (chosen, (own1, at1, to1), (own2, at2, to2)) in enumerate(families):
        for step in steps:
            mail.got(
                gathered.at[core, own1, chosen, rows_of(at2(-step), quarter)],
                tickets[index, step],
            )
        mine = gathered.at[core, own1, chosen]
        for step in steps:
            tickets[index, step] = mail.push(mine, mine, to1(step))
        back[index, 0] = mail.push(mine, mine, place.sibling())
    for step in (1, 3, 2):
        for index, (chosen, (own1, at1, to1), _) in enumerate(families):
            theirs = gathered.at[core, at1(-step), chosen]
            mail.got(theirs, tickets[index, step])
            back[index, step] = mail.push(theirs, theirs, place.sibling())

    for step in (0, 1, 3, 2):
        for index, (chosen, (own1, at1, to1), _) in enumerate(families):
            mail.got(gathered.at[other, at1(-step), chosen], back[index, step])
    mail.finish()


def body(
    student_image,
    student_proj,
    student_text,
    teacher_image,
    teacher_proj,
    teacher_text,
    assignment,
    pair_ids,
):
    per_device, width = student_text.shape
    teacher_width = teacher_text.shape[1]
    student_width = student_image.shape[1]
    features, proj_width = teacher_proj.shape
    size = 128
    kinds = student_width // (2 * size)
    pieces = width // size
    bf16, f32, i32 = jnp.bfloat16, jnp.float32, jnp.int32
    tile = (8, per_device)
    chunk = ring * per_device
    images = n_col * per_device
    hbm = pl.BlockSpec(memory_space=pl.ANY)
    vmem = pl.BlockSpec(memory_space=pltpu.VMEM)
    copies = 236
    grad_embed, gathered = pl.pallas_call(
        step_kernel,
        out_shape=(
            jax.ShapeDtypeStruct((per_device, width), f32),
            jax.ShapeDtypeStruct((2, pieces, kinds, size, size), bf16),
        ),
        in_specs=[hbm] * 8,
        out_specs=[vmem] * 2,
        scratch_shapes=[
            pltpu.VMEM(student_image.shape, bf16),
            pltpu.VMEM(student_proj.shape, bf16),
            pltpu.VMEM(student_text.shape, bf16),
            pltpu.VMEM((features, n_row * per_device), bf16),
            pltpu.VMEM(teacher_text.shape, bf16),
            pltpu.VMEM((ring, ring, per_device, teacher_width + width), bf16),
            pltpu.VMEM((n_col, per_device, width), bf16),
            pltpu.VMEM((n_col, per_device, teacher_width), bf16),
            pltpu.VMEM((n_col, 1, per_device), i32),
            pltpu.VMEM((per_device, width), f32),
            pltpu.VMEM((n_row, 1, per_device), i32),
            pltpu.VMEM((n_row, per_device, features), bf16),
            pltpu.VMEM((n_row, per_device, features), bf16),
            pltpu.VMEM((n_col, n_row, proj_width, features), bf16),
            pltpu.VMEM((teacher_width, per_device), f32),
            pltpu.VMEM((2, ring, images, chunk), f32),
            pltpu.VMEM((2, images, per_device), f32),
            pltpu.VMEM((2, images, per_device), f32),
            pltpu.VMEM((8, chunk), f32),
            pltpu.VMEM((8, chunk), f32),
            pltpu.VMEM((n_col,) + tile, f32),
            pltpu.VMEM((n_col,) + tile, f32),
            pltpu.VMEM((n_col,) + tile, f32),
            pltpu.VMEM((ring, ring) + tile, f32),
            pltpu.VMEM((ring, ring) + tile, f32),
            pltpu.VMEM((ring, ring) + tile, f32),
            pltpu.VMEM((2, images, per_device), f32),
            pltpu.VMEM((images, per_device), i32),
            pltpu.VMEM((ring, 2, per_device, width), f32),
            pltpu.VMEM((ring, per_device, width), f32),
            pltpu.VMEM((ring - 1, per_device, width), bf16),
            pltpu.VMEM((ring - 1, per_device, width), bf16),
            pltpu.VMEM((per_device, student_width // 2), bf16),
            pltpu.VMEM((per_device, width), bf16),
            pltpu.VMEM((per_device, width), bf16),
            pltpu.VMEM((pieces, kinds, size, size), f32),
            pltpu.VMEM((pieces, kinds, size, size), bf16),
            pltpu.VMEM((ring - 1, kinds, size, size), bf16),
            pltpu.VMEM((kinds, size, size), f32),
            pltpu.VMEM((kinds, size, size), bf16),
            pltpu.VMEM((ring - 1, kinds, size // 4, size), bf16),
            pltpu.VMEM((kinds, size // 4, size), f32),
            pltpu.VMEM((ring - 1, kinds, 8, size), f32),
            pltpu.VMEM((2, kinds, size // 4, size), f32),
            pltpu.SemaphoreType.DMA((8,)),
            pltpu.SemaphoreType.DMA((96,)),
            pltpu.SemaphoreType.DMA((copies,)),
        ],
        compiler_params=pltpu.CompilerParams(
            collective_id=0, has_side_effects=True, vmem_limit_bytes=60 * 1024 * 1024
        ),
    )(
        student_image,
        student_proj,
        student_text,
        teacher_image.T,
        teacher_proj.T,
        teacher_text,
        assignment,
        pair_ids,
    )
    grad_proj = gathered.transpose(0, 2, 3, 1, 4).reshape(student_width, width)
    return grad_embed, grad_proj.astype(f32)


def solution(mesh):
    placed = (
        P(("group", "row", "col"), None),
        P(),
        P(("group", "row", "col"), None),
        P(("group", "col"), "row"),
        P("row", "col"),
        P(("group", "row", "col"), None),
        P("group", ("row", "col")),
        P("group", ("row", "col")),
    )
    return jax.shard_map(
        body,
        mesh=mesh,
        in_specs=placed,
        out_specs=(P(("group", "row", "col"), None), P()),
        check_vma=False,
    )
```
